256 devices in a mesh: grp: 2 (over core), gx: 32 (over z, y), gy: 4 (over x).
Axes of the slice: x: 4, y: 4, z: 8, core: 2. Of those that a mesh axis runs over, the one named last changes fastest.
Arguments:
- gas_state: float32 [5, 256, 96, 512], P(None, 'gx', 'grp', 'gy'), may hold values from -0.5 to 3.5, as said below
- droplets: float32 [8, 4194304], P(None, ('grp', 'gx', 'gy')), may hold values from -1 to 7, as said below
- bin_blocks: int32 [32768], P(('grp', 'gx', 'gy')), may hold values from 0 to 95, as said below
- bin_counts: int32 [32768], P(('grp', 'gx', 'gy')), may hold values from 16 to 128, as said below
- crossing: int32 [2, 65536], P(None, ('grp', 'gx', 'gy')), may hold values from 0 to 16383, as said below
Outputs:
- gas_next: float32 [5, 256, 96, 512], P(None, 'gx', 'grp', 'gy')
- droplets_next: float32 [8, 4194304], P(None, ('grp', 'gx', 'gy'))
- arrivals: float32 [8, 2, 65536], P(None, None, ('grp', 'gx', 'gy'))
The draws below stay inside these ranges and needn't reach their ends.
Inputs may be any that keep to these rules, and one draw needn't show every extreme that they name: `gas_state`: component 0 (density) lies in [0.8, 1.2], components 1 to 3 in [-0.5, 0.5], component 4 in [2.5, 3.5]. `droplets`: rows 0 to 2 lie in [0, 7], rows 3 to 5 in [-1, 1], row 6 in [0.5, 2], row 7 in [0.5, 1.5], in every slot. `bin_blocks`: the 4 entries of one device for one gx slab are distinct. `bin_counts`: every device has a bin with 128 live droplets. `crossing`: all 512 entries of one device are distinct slots of live droplets.
All inputs are finite; a program needn't handle non-finite values.
Results may differ from the reference program's by a relative error of at most 0.00014.
Values sent between devices are 32-bit elements; how exact they have to be, the bound alone decides.
No kernel may reach another device: no remote copies, remote signals or barrier semaphores. Data moves between devices by JAX's collectives and lax.ppermute only.
A program may use at most 128 MiB of HBM per device.

```python
import jax
import jax.numpy as jnp
from jax import lax

CX = 8
CZ = 48
CY = 128
NBIN = 128
BINCAP = 128
MIG = 256
CAPB = 4
BLK_DEV = 96
DROP_DEV = 16384
NX = 256
NZ = 96
NY = 512
N_GRP = 2
N_GX = 32
N_GY = 4
DEVICES = 256


def count_table(key):
    subkeys = jax.random.split(key, 3)
    level = jax.random.randint(subkeys[0], (DEVICES, 1), 1, 5)
    counted = jax.random.randint(subkeys[1], (DEVICES, NBIN), BINCAP // 2, BINCAP + 1) * level // 4
    full_bin = jax.random.randint(subkeys[2], (DEVICES, 1), 0, NBIN)
    bin_index = jnp.arange(NBIN, dtype=jnp.int32)[None, :]
    return jnp.where(bin_index == full_bin, BINCAP, counted).astype(jnp.int32)


def draw_gas_state(key, part):
    key = jax.random.fold_in(key, 11)
    subkeys = jax.random.split(key, 3)
    grid_shape = (NX, NZ, NY)
    density = jax.random.uniform(subkeys[0], (1,) + grid_shape, jnp.float32, 0.8, 1.2)
    momentum = jax.random.uniform(subkeys[1], (3,) + grid_shape, jnp.float32, -0.5, 0.5)
    energy = jax.random.uniform(subkeys[2], (1,) + grid_shape, jnp.float32, 2.5, 3.5)
    return jnp.concatenate([density, momentum, energy], axis=0)


def draw_droplets(key, part):
    key = jax.random.fold_in(key, 12)
    subkeys = jax.random.split(key, 4)
    total = DEVICES * DROP_DEV
    position = jax.random.uniform(subkeys[0], (3, total), jnp.float32, 0.0, 7.0)
    velocity = jax.random.uniform(subkeys[1], (3, total), jnp.float32, -1.0, 1.0)
    droplet_mass = jnp.exp(jax.random.uniform(subkeys[2], (1, total), jnp.float32, -0.6931, 0.6931))
    droplet_heat = jax.random.uniform(subkeys[3], (1, total), jnp.float32, 0.5, 1.5)
    return jnp.concatenate([position, velocity, droplet_mass, droplet_heat], axis=0)


def draw_bin_blocks(key, part):
    key = jax.random.fold_in(key, 13)
    scores = jax.random.randint(key, (DEVICES * N_GX, BLK_DEV), 0, 2 ** 14) * BLK_DEV + jnp.arange(BLK_DEV, dtype=jnp.int32)[None, :]
    ordering = jnp.argsort(scores, axis=1)
    return ordering[:, :CAPB].astype(jnp.int32).reshape(DEVICES * NBIN)


def draw_bin_counts(key, part):
    table = count_table(key)
    return table.reshape(DEVICES * NBIN)


def draw_crossing(key, part):
    table = count_table(key)
    key = jax.random.fold_in(key, 19)
    slot_index = jnp.arange(BINCAP, dtype=jnp.int32)
    alive = (slot_index[None, None, :] < table[:, :, None]).reshape(DEVICES, DROP_DEV)
    position = jnp.arange(DROP_DEV, dtype=jnp.int32)[None, :]
    scores = jax.random.randint(key, (DEVICES, DROP_DEV), 0, 2 ** 10) * DROP_DEV + position
    scores = jnp.where(alive, scores, 2 ** 10 * DROP_DEV + position)
    ordering = jnp.argsort(scores, axis=1)[:, :2 * MIG].astype(jnp.int32)
    return ordering.reshape(DEVICES, 2, MIG).transpose(1, 0, 2).reshape(2, DEVICES * MIG)


def setup_inputs(seed: int = 0) -> dict:
    arg_keys = jax.random.split(jax.random.key(seed), 6)
    gas_state = draw_gas_state(jax.random.fold_in(arg_keys[5], 71), 0)
    droplets = draw_droplets(jax.random.fold_in(arg_keys[5], 71), 0)
    bin_blocks = draw_bin_blocks(jax.random.fold_in(arg_keys[5], 71), 0)
    bin_counts = draw_bin_counts(jax.random.fold_in(arg_keys[5], 71), 0)
    crossing = draw_crossing(jax.random.fold_in(arg_keys[5], 71), 0)
    return {"gas_state": gas_state, "droplets": droplets, "bin_blocks": bin_blocks, "bin_counts": bin_counts, "crossing": crossing}


gamma_minus = 0.4
wave_speed = 3.0
step_ratio = 0.1
time_step = 0.2
drag_time = 0.25
evap_rate = 1.0
heat_ratio = 1.5
liquid_heat = 1.0
parcel_weight = 4.0
bins_per_group = 16


def physical_flux(state, direction):
    density = state[0]
    velocity = state[1:4] / density
    pressure = gamma_minus * (state[4] - 0.5 * jnp.sum(state[1:4] * velocity, axis=0))
    normal_speed = velocity[direction]
    pieces = [state[0] * normal_speed]
    for part_index in range(3):
        if part_index == direction:
            pieces.append(state[1 + part_index] * normal_speed + pressure)
        else:
            pieces.append(state[1 + part_index] * normal_speed)
    pieces.append((state[4] + pressure) * normal_speed)
    return jnp.stack(pieces)


def crop_other(field, keep_along):
    for other in (1, 2, 3):
        if other != keep_along:
            field = lax.slice_in_dim(field, 1, field.shape[other] - 1, axis=other)
    return field


def divergence(padded):
    summed = None
    for direction in range(3):
        along = direction + 1
        stripe = crop_other(padded, along)
        fluxes = physical_flux(stripe, direction)
        extent = stripe.shape[along]
        lower_cells = lax.slice_in_dim(stripe, 0, extent - 1, axis=along)
        upper_cells = lax.slice_in_dim(stripe, 1, extent, axis=along)
        lower_flux = lax.slice_in_dim(fluxes, 0, extent - 1, axis=along)
        upper_flux = lax.slice_in_dim(fluxes, 1, extent, axis=along)
        face_flux = 0.5 * (lower_flux + upper_flux) - (0.5 * wave_speed) * (upper_cells - lower_cells)
        change = lax.slice_in_dim(face_flux, 1, extent - 1, axis=along) - lax.slice_in_dim(face_flux, 0, extent - 2, axis=along)
        summed = change if summed is None else summed + change
    return summed


def hat_weights(position):
    node_points = jnp.arange(8, dtype=jnp.float32)[:, None]
    hat_values = jnp.maximum(0.0, 1.0 - jnp.abs(position[:, :, None, :] - node_points))
    product = hat_values[0][:, :, None, None, :] * hat_values[1][:, None, :, None, :] * hat_values[2][:, None, None, :, :]
    return product.reshape(position.shape[1], 512, position.shape[2])


def droplet_update(sampled, state):
    density = sampled[0]
    gas_velocity = sampled[1:4] / density
    pressure = gamma_minus * (sampled[4] - 0.5 * jnp.sum(sampled[1:4] * gas_velocity, axis=0))
    gas_heat = pressure / density
    position = state[0:3]
    velocity = state[3:6]
    droplet_mass = state[6]
    droplet_heat = state[7]
    surface = jnp.power(droplet_mass, 2.0 / 3.0)
    response = drag_time * surface / density
    velocity_new = gas_velocity + (velocity - gas_velocity) * jnp.exp(-time_step / response)
    mass_new = droplet_mass * jnp.exp(-time_step * evap_rate * gas_heat * droplet_heat / surface)
    heat_new = gas_heat + (droplet_heat - gas_heat) * jnp.exp(-time_step / (heat_ratio * response))
    position_new = position + time_step * velocity_new
    mass_gain = droplet_mass - mass_new
    momentum_gain = droplet_mass * velocity - mass_new * velocity_new
    energy_gain = (0.5 * droplet_mass * jnp.sum(velocity * velocity, axis=0) + liquid_heat * droplet_mass * droplet_heat
                   - 0.5 * mass_new * jnp.sum(velocity_new * velocity_new, axis=0) - liquid_heat * mass_new * heat_new)
    new_state = jnp.concatenate([position_new, velocity_new, mass_new[None], heat_new[None]], axis=0)
    gains = jnp.concatenate([mass_gain[None], momentum_gain, energy_gain[None]], axis=0)
    return new_state, gains


def spray_bins(gas_bins, droplet_state, alive):
    bin_total = gas_bins.shape[0]
    capacity = alive.shape[1]
    groups = bin_total // bins_per_group
    gas_groups = gas_bins.reshape(groups, bins_per_group, 5, 512)
    state_groups = droplet_state.reshape(8, groups, bins_per_group, capacity).transpose(1, 0, 2, 3)
    alive_groups = alive.reshape(groups, bins_per_group, capacity)

    def per_group(inputs):
        gas_part, state_part, alive_part = inputs
        weights = hat_weights(state_part[0:3])
        sampled = jnp.einsum('gvn,gnc->vgc', gas_part, weights, precision=lax.Precision.HIGHEST)
        new_state, gains = droplet_update(sampled, state_part)
        gains = gains * (parcel_weight * alive_part)
        deposit = jnp.einsum('vgc,gnc->gvn', gains, weights, precision=lax.Precision.HIGHEST)
        return new_state, deposit

    new_groups, deposit_groups = lax.map(per_group, (gas_groups, state_groups, alive_groups))
    return new_groups.transpose(1, 0, 2, 3).reshape(8, bin_total * capacity), deposit_groups.reshape(bin_total, 5, 512)


def reference(gas_state, droplets, bin_blocks, bin_counts, crossing):
    device_total = N_GRP * N_GX * N_GY
    padded = jnp.pad(gas_state, ((0, 0), (1, 1), (1, 1), (1, 1)), mode="wrap")

    def slab_flow(slab_index):
        piece = lax.dynamic_slice_in_dim(padded, slab_index * CX, CX + 2, axis=1)
        return divergence(piece)

    flow = lax.map(slab_flow, jnp.arange(N_GX, dtype=jnp.int32))
    flow = flow.transpose(1, 0, 2, 3, 4).reshape(5, NX, NZ, NY)

    z_blocks = NZ // 8
    y_blocks = NY // 8
    all_blocks = gas_state.reshape(5, NX // 8, 8, z_blocks, 8, y_blocks, 8).transpose(1, 3, 5, 0, 2, 4, 6).reshape(-1, 5, 512)
    device_index = jnp.arange(device_total, dtype=jnp.int32)[:, None]
    bin_index = jnp.arange(NBIN, dtype=jnp.int32)[None, :]
    local_ids = bin_blocks.reshape(device_total, NBIN)
    block_x = (bin_index // CAPB) * (CX // 8) + local_ids // ((CZ // 8) * (CY // 8))
    block_z = (device_index // (N_GX * N_GY)) * (CZ // 8) + (local_ids // (CY // 8)) % (CZ // 8)
    block_y = (device_index % N_GY) * (CY // 8) + local_ids % (CY // 8)
    global_ids = ((block_x * z_blocks + block_z) * y_blocks + block_y).astype(jnp.int32)
    slot_index = jnp.arange(BINCAP, dtype=jnp.int32)
    alive = (slot_index[None, None, :] < bin_counts.reshape(device_total, NBIN)[:, :, None]).astype(jnp.float32)
    device_drops = droplets.reshape(8, device_total, DROP_DEV).transpose(1, 0, 2)

    def per_device(inputs):
        block_ids, state, alive_part = inputs
        return spray_bins(jnp.take(all_blocks, block_ids, axis=0), state, alive_part)

    updated, deposit = lax.map(per_device, (global_ids, device_drops, alive))
    block_sums = jax.ops.segment_sum(deposit.reshape(-1, 2560), global_ids.reshape(-1), num_segments=all_blocks.shape[0])
    cell_sources = block_sums.reshape(NX // 8, z_blocks, y_blocks, 5, 8, 8, 8).transpose(3, 0, 4, 1, 5, 2, 6).reshape(5, NX, NZ, NY)
    gas_next = gas_state - step_ratio * flow + cell_sources

    leaving_slots = crossing.reshape(2, device_total, MIG).transpose(1, 0, 2)

    def departed_mask(slots):
        return jnp.zeros((DROP_DEV,), jnp.float32).at[slots.reshape(-1)].set(1.0)

    departed = jax.vmap(departed_mask)(leaving_slots)
    keep_mask = alive.reshape(device_total, DROP_DEV) * (1.0 - departed)
    droplets_next = (updated * keep_mask[:, None, :]).transpose(1, 0, 2).reshape(8, device_total * DROP_DEV)

    def pick_leaving(state, slots):
        return jnp.take(state, slots, axis=1)

    leaving = jax.vmap(pick_leaving)(updated, leaving_slots)
    leaving = leaving.reshape(N_GRP, N_GX, N_GY, 8, 2, MIG)
    from_previous = jnp.roll(leaving[:, :, :, :, 0, :], 1, axis=1)
    from_next = jnp.roll(leaving[:, :, :, :, 1, :], -1, axis=1)
    arriving = jnp.stack([from_previous, from_next], axis=4)
    arrivals = arriving.transpose(3, 4, 0, 1, 2, 5).reshape(8, 2, device_total * MIG)
    return gas_next, droplets_next, arrivals
```

```python
import jax
import jax.numpy as jnp
from jax import lax
from jax.experimental import pallas as pl
from jax.experimental.pallas import tpu as pltpu
from jax.sharding import PartitionSpec as P

f32 = jnp.float32
bf16 = jnp.bfloat16

peers = 32
per_peer = 4
bins = 128
lanes = 128
blocks = 96
depth, across, height = 8, 48, 128
plane = depth * across
chunk_rows = per_peer * 8 + 1
moving = 256

vmem = pl.BlockSpec(memory_space=pltpu.VMEM)
smem = pl.BlockSpec(memory_space=pltpu.SMEM)


def params(mib):
    return pltpu.CompilerParams(vmem_limit_bytes=mib * 1024 * 1024)


def lane_index(rows):
    return lax.broadcasted_iota(jnp.int32, (rows, lanes), 1)


def split(x):
    high = x.astype(bf16)
    return high, (x - high.astype(f32)).astype(bf16)


def pack_kernel(drops, ids, counts, out):
    lane = lane_index(1)
    for p in range(peers):
        out[p * chunk_rows : p * chunk_rows + 32, :] = drops[p * 32 : (p + 1) * 32, :]
        row = jnp.zeros((1, lanes), jnp.int32)
        for r in range(per_peer):
            row = jnp.where(lane == r, ids[p * per_peer + r], row)
            row = jnp.where(lane == per_peer + r, counts[p * per_peer + r], row)
        out[p * chunk_rows + 32 : (p + 1) * chunk_rows, :] = row.astype(f32)


def face_kernel(gas, x_low, x_high, z_both, y_low, y_high):
    for v in range(5):
        x_low[v * across : (v + 1) * across, :] = gas[v * plane : v * plane + across, :]
        x_high[v * across : (v + 1) * across, :] = gas[(v + 1) * plane - across : (v + 1) * plane, :]
        z_both[v * 8 : (v + 1) * 8, :] = gas[pl.ds(v * plane, 8, stride=across), :]
        z_both[40 + v * 8 : 40 + (v + 1) * 8, :] = gas[pl.ds(v * plane + across - 1, 8, stride=across), :]
    row = lax.broadcasted_iota(jnp.int32, (8, lanes), 0)
    lane = lane_index(8)
    pick = jnp.where((row == 0) & (lane == 0) | (row == 1) & (lane == lanes - 1), 1.0, 0.0).astype(f32)
    ends = lax.dot_general(
        pick, gas[...], (((1,), (1,)), ((), ())),
        precision=lax.Precision.HIGHEST, preferred_element_type=f32,
    )
    y_low[...] = ends[0:1]
    y_high[...] = ends[1:2]


def table_kernel(gas, out, padded):
    padded[0 : 5 * plane, :] = gas[...]
    padded[5 * plane :, :] = jnp.zeros((3 * plane, lanes), f32)
    lane = lane_index(64)
    group = (lane >> 3) & 7
    first = lane < 64

    def strip(bz, carry):
        for by in range(8):
            pair = jnp.zeros((64, lanes), f32)
            for j in range(8):
                tiles = [
                    padded[pl.ds(i * across + bz * 8 + j, 8, stride=plane), :] for i in range(8)
                ]
                layer = jnp.concatenate(tiles, axis=0)
                shift = (j - by) * 8 % lanes
                if shift:
                    layer = pltpu.roll(layer, shift, 1)
                pair = jnp.where(group == j, layer, pair)
            other = pltpu.roll(pair, 64, 1)
            for number, block in ((by, jnp.where(first, pair, other)), (by + 8, jnp.where(first, other, pair))):
                high, low = split(block)
                start = pl.multiple_of((bz * 16 + number) * 128, 128)
                out[pl.ds(start, 64), :] = high
                out[pl.ds(start + 64, 64), :] = low
        return carry

    lax.fori_loop(0, 6, strip, 0)


def hats(tile):
    node = lax.broadcasted_iota(jnp.int32, (8, lanes), 0).astype(f32)
    return [jnp.maximum(0.0, 1.0 - jnp.abs(tile[a : a + 1] - node)) for a in range(3)]


def pair_weights(hat_z, hat_y):
    high, low = split(jnp.concatenate([hat_z[j : j + 1] * hat_y for j in range(8)], axis=0))
    return jnp.concatenate([high, low], axis=0)


def sample_kernel(received, table, results, drops, index, index_smem, sampled, sem):
    for p in range(peers):
        index[p : p + 1, :] = received[p * chunk_rows + 32 : (p + 1) * chunk_rows, :].astype(jnp.int32)
    copy = pltpu.make_async_copy(index, index_smem, sem)
    copy.start()
    for p in range(peers):
        drops[p * 32 : (p + 1) * 32, :] = received[p * chunk_rows : p * chunk_rows + 32, :]
    copy.wait()

    def group(g, carry):
        base = pl.multiple_of(g * 64, 64)
        for b in range(8):
            hat_x, hat_z, hat_y = hats(drops[pl.ds(base + b * 8, 8), :])
            block = index_smem[g * 2 + b // 4, b % 4]
            rows = table[pl.ds(pl.multiple_of(block * 128, 128), 128), :]
            product = jnp.dot(rows, pair_weights(hat_z, hat_y), preferred_element_type=f32)
            total = None
            for i in range(8):
                part = (product[i * 8 : i * 8 + 8] + product[64 + i * 8 : 72 + i * 8]) * hat_x[i : i + 1]
                total = part if total is None else total + part
            sampled[b * 8 : (b + 1) * 8, :] = total
        density, m1, m2, m3, energy = [sampled[pl.ds(v, 8, stride=8), :] for v in range(5)]
        v1, v2, v3, mass, heat = [drops[pl.ds(base + n, 8, stride=8), :] for n in range(3, 8)]
        inverse = 1.0 / density
        u1, u2, u3 = m1 * inverse, m2 * inverse, m3 * inverse
        gas_heat = 0.4 * (energy - 0.5 * (m1 * u1 + m2 * u2 + m3 * u3)) * inverse
        inverse_area = jnp.exp(jnp.log(mass) * (-2.0 / 3.0))
        rate = density * inverse_area * -0.8
        drag = jnp.exp(rate)
        values = [
            u1 + (v1 - u1) * drag,
            u2 + (v2 - u2) * drag,
            u3 + (v3 - u3) * drag,
            mass * jnp.exp(-0.2 * gas_heat * heat * inverse_area),
            gas_heat + (heat - gas_heat) * jnp.exp(rate * (1.0 / 1.5)),
        ]
        for n in range(5):
            results[pl.ds(g * 40 + n, 8, stride=5), :] = values[n]
        return carry

    lax.fori_loop(0, bins // 8, group, 0)


def primitives(s):
    inverse = 1.0 / s[0]
    u = [s[1] * inverse, s[2] * inverse, s[3] * inverse]
    pressure = 0.4 * (s[4] - 0.5 * (s[1] * u[0] + s[2] * u[1] + s[3] * u[2]))
    return u, pressure


def flux(s, u, pressure, a):
    normal = u[a]
    out = [s[1 + a]]
    for c in range(3):
        out.append(s[1 + c] * normal + pressure if c == a else s[1 + c] * normal)
    out.append((s[4] + pressure) * normal)
    return out


def gas_kernel(results, drops, index, gas, x_low, x_high, z_both, y_low, y_high, out,
               sums, gains, pairs, sources, y_ends, x_padded, z_flux):
    sums[...] = jnp.zeros(sums.shape, f32)
    lane8 = lane_index(8)

    def group(g, carry):
        base = pl.multiple_of(g * 64, 64)
        v1, v2, v3, mass, heat = [drops[pl.ds(base + n, 8, stride=8), :] for n in range(3, 8)]
        w1, w2, w3, mass_new, heat_new = [results[pl.ds(g * 40 + n, 8, stride=5), :] for n in range(5)]
        values = [
            mass - mass_new,
            mass * v1 - mass_new * w1,
            mass * v2 - mass_new * w2,
            mass * v3 - mass_new * w3,
            0.5 * mass * (v1 * v1 + v2 * v2 + v3 * v3) + mass * heat
            - 0.5 * mass_new * (w1 * w1 + w2 * w2 + w3 * w3) - mass_new * heat_new,
        ]
        for n in range(5):
            gains[pl.ds(n, 8, stride=8), :] = 4.0 * values[n]
        for b in range(8):
            hat_x, hat_z, hat_y = hats(drops[pl.ds(base + b * 8, 8), :])
            peer = g * 2 + b // 4
            block = index[peer, b % 4]
            live = jnp.where(lane8 < index[peer, per_peer + b % 4], gains[b * 8 : (b + 1) * 8, :], 0.0)
            spread = jnp.concatenate([live[v : v + 1] * hat_x for v in range(5)], axis=0)
            high, low = split(spread)
            weights = pair_weights(hat_z, hat_y)
            dims = (((1,), (1,)), ((), ()))
            added = lax.dot_general(high, weights, dims, preferred_element_type=f32)
            added += lax.dot_general(low, weights, dims, preferred_element_type=f32)
            place = pl.ds(pl.multiple_of(block * 40, 8), 40)
            sums[place, :] = sums[place, :] + added
        return carry

    lax.fori_loop(0, bins // 8, group, 0)

    lane40 = lane_index(40)
    chunk = (lane40 >> 3) & 7
    first = lane40 < 64

    def strip(bz, carry):
        for by in range(8):
            near = sums[pl.ds(pl.multiple_of((bz * 16 + by) * 40, 8), 40), :]
            far = sums[pl.ds(pl.multiple_of((bz * 16 + by + 8) * 40, 8), 40), :]
            pairs[by * 40 : (by + 1) * 40, :] = jnp.where(
                first, near + pltpu.roll(near, 64, 1), far + pltpu.roll(far, 64, 1)
            )
        for j in range(8):
            layer = jnp.zeros((40, lanes), f32)
            for by in range(8):
                part = pairs[by * 40 : (by + 1) * 40, :]
                shift = (by - j) * 8 % lanes
                if shift:
                    part = pltpu.roll(part, shift, 1)
                layer = jnp.where(chunk == by, part, layer)
            for v in range(5):
                sources[pl.ds(v * plane + bz * 8 + j, 8, stride=across), :] = layer[v * 8 : (v + 1) * 8]
        return carry

    lax.fori_loop(0, 6, strip, 0)

    row8 = lax.broadcasted_iota(jnp.int32, (8, lanes), 0)
    place = jnp.where((row8 == 0) & (lane8 == 0) | (row8 == 1) & (lane8 == lanes - 1), 1.0, 0.0).astype(f32)
    ends = jnp.concatenate([y_low[...], y_high[...], jnp.zeros((6, 5 * plane), f32)], axis=0)
    y_ends[...] = lax.dot_general(
        ends, place, (((0,), (0,)), ((), ())),
        precision=lax.Precision.HIGHEST, preferred_element_type=f32,
    )
    for v in range(5):
        x_padded[v * 480 : v * 480 + across, :] = x_low[v * across : (v + 1) * across, :]
        x_padded[v * 480 + across : v * 480 + 432, :] = gas[v * plane : (v + 1) * plane, :]
        x_padded[v * 480 + 432 : (v + 1) * 480, :] = x_high[v * across : (v + 1) * across, :]
    for side in range(2):
        edge = [z_both[side * 40 + v * 8 : side * 40 + (v + 1) * 8, :] for v in range(5)]
        edge_flux = flux(edge, *primitives(edge), 1)
        for v in range(5):
            z_flux[side * 40 + v * 8 : side * 40 + (v + 1) * 8, :] = edge_flux[v]

    row = lax.broadcasted_iota(jnp.int32, (across, lanes), 0)
    lane = lane_index(across)

    def layer(i, carry):
        def cells(at):
            return [x_padded[pl.ds(pl.multiple_of(v * 480 + at * across, 8), across), :] for v in range(5)]

        def rows(v):
            return pl.ds(pl.multiple_of(v * plane + i * across, 8), across)

        here, below, above = cells(i + 1), cells(i), cells(i + 2)
        u, pressure = primitives(here)
        flux_above = flux(above, *primitives(above), 0)
        flux_below = flux(below, *primitives(below), 0)
        flux_z = flux(here, u, pressure, 1)
        flux_y = flux(here, u, pressure, 2)
        ends = [y_ends[rows(v), :] for v in range(5)]
        flux_ends = flux(ends, *primitives(ends), 2)
        for v in range(5):
            z_low = z_both[pl.ds(40 + v * 8 + i, 1), :]
            z_high = z_both[pl.ds(v * 8 + i, 1), :]
            z_low_flux = z_flux[pl.ds(40 + v * 8 + i, 1), :]
            z_high_flux = z_flux[pl.ds(v * 8 + i, 1), :]

            def z_pair(x, low, high):
                return (
                    jnp.where(row == 0, low, pltpu.roll(x, 1, 0)),
                    jnp.where(row == across - 1, high, pltpu.roll(x, across - 1, 0)),
                )

            def y_pair(x, end):
                return (
                    jnp.where(lane == 0, end, pltpu.roll(x, 1, 1)),
                    jnp.where(lane == lanes - 1, end, pltpu.roll(x, lanes - 1, 1)),
                )

            z_down, z_up = z_pair(here[v], z_low, z_high)
            z_flux_down, z_flux_up = z_pair(flux_z[v], z_low_flux, z_high_flux)
            y_down, y_up = y_pair(here[v], ends[v])
            y_flux_down, y_flux_up = y_pair(flux_y[v], flux_ends[v])
            spread = (below[v] + above[v]) + (z_down + z_up) + (y_down + y_up) - 6.0 * here[v]
            change = (flux_above[v] - flux_below[v]) + (z_flux_up - z_flux_down) + (y_flux_up - y_flux_down)
            flow = 0.5 * change - 1.5 * spread
            out[rows(v), :] = here[v] - 0.1 * flow + sources[rows(v), :]
        return carry

    lax.fori_loop(0, depth, layer, 0)


def leave_kernel(returned, drops, crossing, updated, toward_next, toward_previous, shifted):
    shifted[0:8, :] = jnp.zeros((8, lanes), f32)
    shifted[8 : 8 + 640, :] = returned[...]
    shifted[648:656, :] = jnp.zeros((8, lanes), f32)
    row = lax.broadcasted_iota(jnp.int32, (8, lanes), 0)
    for b in range(bins):
        speeds = shifted[8 + b * 5 : 16 + b * 5, :]
        values = shifted[5 + b * 5 : 13 + b * 5, :]
        updated[b * 8 : (b + 1) * 8, :] = jnp.where(row < 3, drops[b * 8 : (b + 1) * 8, :] + 0.2 * speeds, values)

    lane = lane_index(8)

    def batch(s, carry):
        tiles = list(carry)
        for t in range(4):
            for e in range(8):
                target = s * 8 + e
                slot = crossing[t // 2, (t % 2) * lanes + target]
                tile = updated[pl.ds(pl.multiple_of((slot >> 7) * 8, 8), 8), :]
                moved = pltpu.roll(tile, (target - slot) & (lanes - 1), 1)
                tiles[t] = jnp.where(lane == target, moved, tiles[t])
        return tuple(tiles)

    tiles = lax.fori_loop(0, lanes // 8, batch, (jnp.zeros((8, lanes), f32),) * 4)
    toward_next[...] = jnp.concatenate(tiles[0:2], axis=1)
    toward_previous[...] = jnp.concatenate(tiles[2:4], axis=1)


def stay_kernel(updated, counts, crossing, out):
    row = lax.broadcasted_iota(jnp.int32, (bins, moving), 0)
    departed = None
    for side in range(2):
        slots = crossing[side : side + 1, :]
        in_bin = jnp.where(row == (slots >> 7), 1.0, 0.0).astype(bf16)
        in_lane = jnp.where(row == (slots & (lanes - 1)), 1.0, 0.0).astype(bf16)
        part = lax.dot_general(in_bin, in_lane, (((1,), (1,)), ((), ())), preferred_element_type=f32)
        departed = part if departed is None else departed + part
    stays = 1.0 - departed
    lane = lane_index(1)
    for b in range(bins):
        keep = jnp.where(lane < counts[b], stays[b : b + 1], 0.0)
        out[b * 8 : (b + 1) * 8, :] = updated[b * 8 : (b + 1) * 8, :] * keep


def shape(rows, columns=lanes, dtype=f32):
    return jax.ShapeDtypeStruct((rows, columns), dtype)


def shifted_by(x, axis, by):
    count = lax.axis_size(axis)
    return lax.ppermute(x, axis, [(i, (i + by) % count) for i in range(count)])


def exchange(x):
    return lax.all_to_all(x, "gx", split_axis=0, concat_axis=0, tiled=True)


def per_device(gas_state, droplets, bin_blocks, bin_counts, crossing):
    gas = gas_state.reshape(5 * plane, lanes)
    drops = droplets.reshape(8, bins, lanes).transpose(1, 0, 2).reshape(bins * 8, lanes)

    packed = pl.pallas_call(
        pack_kernel, out_shape=shape(peers * chunk_rows), in_specs=[vmem, smem, smem], out_specs=vmem,
        compiler_params=params(16),
    )(drops, bin_blocks, bin_counts)
    received = exchange(packed)

    x_low, x_high, z_both, y_low, y_high = pl.pallas_call(
        face_kernel,
        out_shape=[shape(240), shape(240), shape(80), shape(1, 1920), shape(1, 1920)],
        in_specs=[vmem], out_specs=[vmem] * 5, compiler_params=params(16),
    )(gas)
    halo_x_low = shifted_by(x_high, "gx", 1)
    halo_x_high = shifted_by(x_low, "gx", -1)
    halo_z = shifted_by(z_both, "grp", 1)
    halo_y_low = shifted_by(y_high, "gy", 1)
    halo_y_high = shifted_by(y_low, "gy", -1)

    table = pl.pallas_call(
        table_kernel, out_shape=shape(blocks * 128, dtype=bf16), in_specs=[vmem], out_specs=vmem,
        scratch_shapes=[pltpu.VMEM((8 * plane, lanes), f32)], compiler_params=params(24),
    )(gas)

    results, owned, index = pl.pallas_call(
        sample_kernel,
        out_shape=[shape(bins * 5), shape(bins * 8), shape(peers, dtype=jnp.int32)],
        in_specs=[vmem] * 2, out_specs=[vmem] * 3,
        scratch_shapes=[
            pltpu.SMEM((peers, lanes), jnp.int32), pltpu.VMEM((64, lanes), f32), pltpu.SemaphoreType.DMA,
        ],
        compiler_params=params(24),
    )(received, table)
    returned = exchange(results)

    gas_next = pl.pallas_call(
        gas_kernel,
        out_shape=shape(5 * plane),
        in_specs=[vmem] * 2 + [smem] + [vmem] * 6, out_specs=vmem,
        scratch_shapes=[
            pltpu.VMEM((blocks * 40, lanes), f32), pltpu.VMEM((64, lanes), f32), pltpu.VMEM((320, lanes), f32),
            pltpu.VMEM((5 * plane, lanes), f32), pltpu.VMEM((5 * plane, lanes), f32),
            pltpu.VMEM((2400, lanes), f32), pltpu.VMEM((80, lanes), f32),
        ],
        compiler_params=params(32),
    )(results, owned, index, gas, halo_x_low, halo_x_high, halo_z, halo_y_low, halo_y_high)

    updated, toward_next, toward_previous = pl.pallas_call(
        leave_kernel,
        out_shape=[shape(bins * 8), shape(8, moving), shape(8, moving)],
        in_specs=[vmem, vmem, smem], out_specs=[vmem] * 3,
        scratch_shapes=[pltpu.VMEM((656, lanes), f32)], compiler_params=params(16),
    )(returned, drops, crossing)
    from_previous = shifted_by(toward_next, "gx", 1)
    from_next = shifted_by(toward_previous, "gx", -1)
    arrivals = jnp.stack([from_previous, from_next], axis=1)

    kept = pl.pallas_call(
        stay_kernel, out_shape=shape(bins * 8), in_specs=[vmem, smem, vmem], out_specs=vmem,
        compiler_params=params(16),
    )(updated, bin_counts, crossing)
    droplets_next = kept.reshape(bins, 8, lanes).transpose(1, 0, 2).reshape(8, bins * lanes)
    return gas_next.reshape(gas_state.shape), droplets_next, arrivals


def solution(mesh):
    whole = ("grp", "gx", "gy")
    in_specs = (P(None, "gx", "grp", "gy"), P(None, whole), P(whole), P(whole), P(None, whole))
    out_specs = (P(None, "gx", "grp", "gy"), P(None, whole), P(None, None, whole))
    return jax.shard_map(per_device, mesh=mesh, in_specs=in_specs, out_specs=out_specs, check_vma=False)
```

```python
import jax
import jax.numpy as jnp
from jax import lax
from jax.experimental import pallas as pl
from jax.experimental.pallas import tpu as pltpu
from jax.sharding import PartitionSpec as P

f32 = jnp.float32
bf16 = jnp.bfloat16

peers = 32
per_peer = 4
bins = 128
lanes = 128
blocks = 96
depth, across, height = 8, 48, 128
plane = depth * across
tiles_out = per_peer * 2 + 1
moving = 256
together = 16

vmem = pl.BlockSpec(memory_space=pltpu.VMEM)
smem = pl.BlockSpec(memory_space=pltpu.SMEM)
hbm = pl.BlockSpec(memory_space=pltpu.HBM)


def params(mib):
    return pltpu.CompilerParams(vmem_limit_bytes=mib * 1024 * 1024)


def lane_index(rows):
    return lax.broadcasted_iota(jnp.int32, (rows, lanes), 1)


def split(x):
    high = x.astype(bf16)
    return high, (x - high.astype(f32)).astype(bf16)


def pack_kernel(drops, ids, counts, out, held, numbers, sems):
    copies = [
        pltpu.make_async_copy(drops, held, sems.at[0]),
        pltpu.make_async_copy(ids, numbers.at[0], sems.at[1]),
        pltpu.make_async_copy(counts, numbers.at[1], sems.at[2]),
    ]
    for copy in copies:
        copy.start()
    row = lax.broadcasted_iota(jnp.int32, (4, lanes), 0)
    lane = lane_index(4)
    copies[1].wait()
    copies[2].wait()
    both = jnp.where(row == 0, numbers[0], jnp.where(row == 1, numbers[1], 0)).astype(f32)
    for p in range(peers):
        near = pltpu.roll(both, (lanes - p * per_peer) % lanes, 1) if p else both
        out[p * tiles_out + 8] = jnp.where(lane < per_peer, near, 0.0)
    copies[0].wait()
    for p in range(peers):
        for t in range(8):
            out[p * tiles_out + t] = held[p * 32 + t * 4 : p * 32 + t * 4 + 4, :]


def unpack(held, drops, index, index_smem, sem):
    total = held[8]
    for p in range(1, peers):
        total = total + pltpu.roll(held[p * tiles_out + 8], p * per_peer, 1)
    index[...] = total.astype(jnp.int32)
    copy = pltpu.make_async_copy(index, index_smem, sem)
    copy.start()
    for p in range(peers):
        for t in range(8):
            drops[p * 32 + t * 4 : p * 32 + t * 4 + 4, :] = held[p * tiles_out + t]
    copy.wait()


def face_kernel(gas, x_low, x_high, z_both, y_low, y_high):
    for v in range(5):
        x_low[v * across : (v + 1) * across, :] = gas[v * plane : v * plane + across, :]
        x_high[v * across : (v + 1) * across, :] = gas[(v + 1) * plane - across : (v + 1) * plane, :]
        z_both[v * 8 : (v + 1) * 8, :] = gas[pl.ds(v * plane, 8, stride=across), :]
        z_both[40 + v * 8 : 40 + (v + 1) * 8, :] = gas[pl.ds(v * plane + across - 1, 8, stride=across), :]
    row = lax.broadcasted_iota(jnp.int32, (8, lanes), 0)
    lane = lane_index(8)
    pick = jnp.where((row == 0) & (lane == 0) | (row == 1) & (lane == lanes - 1), 1.0, 0.0).astype(f32)
    ends = lax.dot_general(
        pick, gas[...], (((1,), (1,)), ((), ())),
        precision=lax.Precision.HIGHEST, preferred_element_type=f32,
    )
    y_low[...] = ends[0:1]
    y_high[...] = ends[1:2]


def trade_chunks(tiles, chunk):
    for bit in (1, 2, 4):
        upper = (chunk & bit) != 0
        traded = list(tiles)
        for a in range(8):
            if not a & bit:
                b = a | bit
                traded[a] = jnp.where(upper, pltpu.roll(tiles[b], bit * 8, 1), tiles[a])
                traded[b] = jnp.where(upper, tiles[b], pltpu.roll(tiles[a], lanes - bit * 8, 1))
        tiles = traded
    return tiles


def split_rows(tiles):
    first_high, first_low = split(jnp.concatenate(tiles[0:2], axis=0))
    second_high, second_low = split(jnp.concatenate(tiles[2:4], axis=0))
    last = tiles[4].astype(bf16).astype(f32)
    middle = jnp.concatenate([last, tiles[4] - last], axis=0).astype(bf16)
    return [first_high, second_high, middle, first_low, second_low]


high_rows = (0, 8, 16, 24, 32)
low_rows = (48, 56, 64, 72, 40)
block_rows = 80


def table_kernel(gas, out):
    lane = lane_index(8)
    chunk = lane >> 3
    first = lane < 64

    def strip(bz, carry):
        pairs = []
        for v in range(5):
            layers = [gas[pl.ds(v * plane + bz * 8 + j, 8, stride=across), :] for j in range(8)]
            pairs.append(trade_chunks(layers, chunk))
        for by in range(8):
            here = [pairs[v][by] for v in range(5)]
            other = [pltpu.roll(x, 64, 1) for x in here]
            near = [jnp.where(first, a, b) for a, b in zip(here, other)]
            far = [jnp.where(first, b, a) for a, b in zip(here, other)]
            for number, block in ((by, near), (by + 8, far)):
                start = (bz * 16 + number) * block_rows
                for n, part in enumerate(split_rows(block)):
                    out[pl.ds(pl.multiple_of(start + n * 16, 16), 16), :] = part
        return carry

    lax.fori_loop(0, 6, strip, 0)


def hats(tile):
    node = lax.broadcasted_iota(jnp.int32, (8, lanes), 0).astype(f32)
    return [jnp.maximum(0.0, 1.0 - jnp.abs(tile[a : a + 1] - node)) for a in range(3)]


def pair_weights(hat_z, hat_y):
    high, low = split(jnp.concatenate([hat_z[j : j + 1] * hat_y for j in range(8)], axis=0))
    return jnp.concatenate([high, low], axis=0)


def sample_kernel(received, table, results, held, drops, index, index_smem, products, sem):
    copy = pltpu.make_async_copy(received, held, sem)
    copy.start()
    copy.wait()
    unpack(held, drops, index, index_smem, sem)

    def some_bins(n, carry):
        for e in range(together):
            b = n * together + e
            hat_x, hat_z, hat_y = hats(drops[pl.ds(pl.multiple_of(b * 8, 8), 8), :])
            rows = table[pl.ds(pl.multiple_of(index_smem[0, b] * block_rows, 16), block_rows), :]
            product = jnp.dot(rows, pair_weights(hat_z, hat_y), preferred_element_type=f32)
            for v in range(5):
                h, l = high_rows[v], low_rows[v]
                products[pl.ds(pl.multiple_of(b * 40 + v * 8, 8), 8), :] = (product[h : h + 8] + product[l : l + 8]) * hat_x
        return carry

    lax.fori_loop(0, bins // together, some_bins, 0)

    def some_groups(n, carry):
        for e in range(4):
            g = n * 4 + e
            sampled = []
            for v in range(5):
                terms = [products[pl.ds(g * 320 + v * 8 + i, 8, stride=40), :] for i in range(8)]
                while len(terms) > 1:
                    terms = [a + b for a, b in zip(terms[0::2], terms[1::2])]
                sampled.append(terms[0])
            density, m1, m2, m3, energy = sampled
            v1, v2, v3, mass, heat = [drops[pl.ds(g * 64 + v, 8, stride=8), :] for v in range(3, 8)]
            inverse = 1.0 / density
            u1, u2, u3 = m1 * inverse, m2 * inverse, m3 * inverse
            gas_heat = 0.4 * (energy - 0.5 * (m1 * u1 + m2 * u2 + m3 * u3)) * inverse
            inverse_area = jnp.exp(jnp.log(mass) * (-2.0 / 3.0))
            rate = density * inverse_area * -0.8
            drag = jnp.exp(rate)
            values = [
                u1 + (v1 - u1) * drag,
                u2 + (v2 - u2) * drag,
                u3 + (v3 - u3) * drag,
                mass * jnp.exp(-0.2 * gas_heat * heat * inverse_area),
                gas_heat + (heat - gas_heat) * jnp.exp(rate * (1.0 / 1.5)),
            ]
            for v in range(5):
                results[g * 10 + v] = values[v][0:4]
                results[g * 10 + 5 + v] = values[v][4:8]
        return carry

    lax.fori_loop(0, 4, some_groups, 0)


def group_values(results, g):
    return [jnp.concatenate([results[g * 10 + v], results[g * 10 + 5 + v]], axis=0) for v in range(5)]


def primitives(s):
    inverse = 1.0 / s[0]
    u = [s[1] * inverse, s[2] * inverse, s[3] * inverse]
    pressure = 0.4 * (s[4] - 0.5 * (s[1] * u[0] + s[2] * u[1] + s[3] * u[2]))
    return u, pressure


def flux(s, u, pressure, a):
    normal = u[a]
    out = [s[1 + a]]
    for c in range(3):
        out.append(s[1 + c] * normal + pressure if c == a else s[1 + c] * normal)
    out.append((s[4] + pressure) * normal)
    return out


def deposit_kernel(results, received, out, drops, index, index_smem, sums, gains, sem):
    sums[...] = jnp.zeros(sums.shape, f32)
    unpack(received, drops, index, index_smem, sem)

    def some_groups(n, carry):
        for e in range(4):
            g = n * 4 + e
            v1, v2, v3, mass, heat = [drops[pl.ds(g * 64 + v, 8, stride=8), :] for v in range(3, 8)]
            w1, w2, w3, mass_new, heat_new = group_values(results, g)
            values = [
                mass - mass_new,
                mass * v1 - mass_new * w1,
                mass * v2 - mass_new * w2,
                mass * v3 - mass_new * w3,
                0.5 * mass * (v1 * v1 + v2 * v2 + v3 * v3) + mass * heat
                - 0.5 * mass_new * (w1 * w1 + w2 * w2 + w3 * w3) - mass_new * heat_new,
            ]
            for v in range(5):
                gains[pl.ds(g * 64 + v, 8, stride=8), :] = 4.0 * values[v]
        return carry

    lax.fori_loop(0, 4, some_groups, 0)
    lane8 = lane_index(8)

    def some_bins(n, carry):
        for e in range(together):
            b = n * together + e
            here = pl.ds(pl.multiple_of(b * 8, 8), 8)
            hat_x, hat_z, hat_y = hats(drops[here, :])
            live = jnp.where(lane8 < index_smem[1, b], gains[here, :], 0.0)
            spread = jnp.concatenate(split_rows([live[v : v + 1] * hat_x for v in range(5)]), axis=0)
            added = lax.dot_general(
                spread, pair_weights(hat_z, hat_y), (((1,), (1,)), ((), ())), preferred_element_type=f32
            )
            start = index_smem[0, b] * 40
            for v in range(5):
                h, l = high_rows[v], low_rows[v]
                place = pl.ds(pl.multiple_of(start + v * 8, 8), 8)
                sums[place, :] = sums[place, :] + (added[h : h + 8] + added[l : l + 8])
        return carry

    lax.fori_loop(0, bins // together, some_bins, 0)
    chunk = lane8 >> 3
    first = lane8 < 64

    def strip(bz, carry):
        for v in range(5):
            pairs = []
            for by in range(8):
                near = sums[pl.ds(pl.multiple_of((bz * 16 + by) * 40 + v * 8, 8), 8), :]
                far = sums[pl.ds(pl.multiple_of((bz * 16 + by + 8) * 40 + v * 8, 8), 8), :]
                pairs.append(jnp.where(first, near + pltpu.roll(near, 64, 1), far + pltpu.roll(far, 64, 1)))
            for j, layer in enumerate(trade_chunks(pairs, chunk)):
                out[pl.ds(v * plane + bz * 8 + j, 8, stride=across), :] = layer
        return carry

    lax.fori_loop(0, 6, strip, 0)


def flow_kernel(gas, sources, x_low, x_high, z_both, y_low, y_high, out, y_ends, x_padded, z_flux):
    row8 = lax.broadcasted_iota(jnp.int32, (8, lanes), 0)
    lane8 = lane_index(8)
    place = jnp.where((row8 == 0) & (lane8 == 0) | (row8 == 1) & (lane8 == lanes - 1), 1.0, 0.0).astype(f32)
    ends = jnp.concatenate([y_low[...], y_high[...], jnp.zeros((6, 5 * plane), f32)], axis=0)
    y_ends[...] = lax.dot_general(
        ends, place, (((0,), (0,)), ((), ())),
        precision=lax.Precision.HIGHEST, preferred_element_type=f32,
    )
    for v in range(5):
        x_padded[v * 480 : v * 480 + across, :] = x_low[v * across : (v + 1) * across, :]
        x_padded[v * 480 + across : v * 480 + 432, :] = gas[v * plane : (v + 1) * plane, :]
        x_padded[v * 480 + 432 : (v + 1) * 480, :] = x_high[v * across : (v + 1) * across, :]
    for side in range(2):
        edge = [z_both[side * 40 + v * 8 : side * 40 + (v + 1) * 8, :] for v in range(5)]
        edge_flux = flux(edge, *primitives(edge), 1)
        for v in range(5):
            z_flux[side * 40 + v * 8 : side * 40 + (v + 1) * 8, :] = edge_flux[v]

    row = lax.broadcasted_iota(jnp.int32, (across, lanes), 0)
    lane = lane_index(across)

    def layer(i, carry):
        def cells(at):
            return [x_padded[pl.ds(pl.multiple_of(v * 480 + at * across, 8), across), :] for v in range(5)]

        def rows(v):
            return pl.ds(pl.multiple_of(v * plane + i * across, 8), across)

        here, below, above = cells(i + 1), cells(i), cells(i + 2)
        u, pressure = primitives(here)
        flux_above = flux(above, *primitives(above), 0)
        flux_below = flux(below, *primitives(below), 0)
        flux_z = flux(here, u, pressure, 1)
        flux_y = flux(here, u, pressure, 2)
        ends = [y_ends[rows(v), :] for v in range(5)]
        flux_ends = flux(ends, *primitives(ends), 2)
        for v in range(5):
            z_low = z_both[pl.ds(40 + v * 8 + i, 1), :]
            z_high = z_both[pl.ds(v * 8 + i, 1), :]
            z_low_flux = z_flux[pl.ds(40 + v * 8 + i, 1), :]
            z_high_flux = z_flux[pl.ds(v * 8 + i, 1), :]

            def z_pair(x, low, high):
                return (
                    jnp.where(row == 0, low, pltpu.roll(x, 1, 0)),
                    jnp.where(row == across - 1, high, pltpu.roll(x, across - 1, 0)),
                )

            def y_pair(x, end):
                return (
                    jnp.where(lane == 0, end, pltpu.roll(x, 1, 1)),
                    jnp.where(lane == lanes - 1, end, pltpu.roll(x, lanes - 1, 1)),
                )

            z_down, z_up = z_pair(here[v], z_low, z_high)
            z_flux_down, z_flux_up = z_pair(flux_z[v], z_low_flux, z_high_flux)
            y_down, y_up = y_pair(here[v], ends[v])
            y_flux_down, y_flux_up = y_pair(flux_y[v], flux_ends[v])
            spread = (below[v] + above[v]) + (z_down + z_up) + (y_down + y_up) - 6.0 * here[v]
            change = (flux_above[v] - flux_below[v]) + (z_flux_up - z_flux_down) + (y_flux_up - y_flux_down)
            flow = 0.5 * change - 1.5 * spread
            out[rows(v), :] = here[v] - 0.1 * flow + sources[rows(v), :]
        return carry

    lax.fori_loop(0, depth, layer, 0)


def leave_kernel(returned, drops, crossing, updated, toward_next, toward_previous):
    for g in range(bins // 8):
        values = group_values(returned, g)
        for v in range(5):
            updated[pl.ds(g * 64 + 3 + v, 8, stride=8), :] = values[v]
        for a in range(3):
            at = pl.ds(g * 64 + a, 8, stride=8)
            updated[at, :] = drops[at, :] + 0.2 * values[a]

    lane = lane_index(8)

    def batch(s, carry):
        tiles = list(carry)
        for t in range(4):
            for e in range(8):
                target = s * 8 + e
                slot = crossing[t // 2, (t % 2) * lanes + target]
                tile = updated[pl.ds(pl.multiple_of((slot >> 7) * 8, 8), 8), :]
                moved = pltpu.roll(tile, (target - slot) & (lanes - 1), 1)
                tiles[t] = jnp.where(lane == target, moved, tiles[t])
        return tuple(tiles)

    tiles = lax.fori_loop(0, lanes // 8, batch, (jnp.zeros((8, lanes), f32),) * 4)
    toward_next[...] = jnp.concatenate(tiles[0:2], axis=1)
    toward_previous[...] = jnp.concatenate(tiles[2:4], axis=1)


def stay_kernel(updated, counts, crossing, out):
    row = lax.broadcasted_iota(jnp.int32, (bins, moving), 0)
    departed = None
    for side in range(2):
        slots = crossing[side : side + 1, :]
        in_bin = jnp.where(row == (slots >> 7), 1.0, 0.0).astype(bf16)
        in_lane = jnp.where(row == (slots & (lanes - 1)), 1.0, 0.0).astype(bf16)
        part = lax.dot_general(in_bin, in_lane, (((1,), (1,)), ((), ())), preferred_element_type=f32)
        departed = part if departed is None else departed + part
    stays = 1.0 - departed
    lane = lane_index(1)
    for b in range(bins):
        keep = jnp.where(lane < counts[b], stays[b : b + 1], 0.0)
        out[b * 8 : (b + 1) * 8, :] = updated[b * 8 : (b + 1) * 8, :] * keep


def shape(rows, columns=lanes, dtype=f32):
    return jax.ShapeDtypeStruct((rows, columns), dtype)


def shifted_by(x, axis, by):
    count = lax.axis_size(axis)
    return lax.ppermute(x, axis, [(i, (i + by) % count) for i in range(count)])


def exchange(x):
    return lax.all_to_all(x, "gx", split_axis=0, concat_axis=0, tiled=True)


def call(kernel, out_shape, in_specs, mib, scratch=()):
    one = not isinstance(out_shape, list)
    return pl.pallas_call(
        kernel, name=kernel.__name__, out_shape=out_shape, in_specs=in_specs,
        out_specs=vmem if one else [vmem] * len(out_shape),
        scratch_shapes=list(scratch), compiler_params=params(mib),
    )


def pack(drops, bin_blocks, bin_counts):
    return call(
        pack_kernel, jax.ShapeDtypeStruct((peers * tiles_out, 4, lanes), f32), [hbm] * 3, 60,
        [pltpu.VMEM((bins * 8, lanes), f32), pltpu.VMEM((2, 1, lanes), jnp.int32), pltpu.SemaphoreType.DMA((3,))],
    )(drops, bin_blocks.reshape(1, bins), bin_counts.reshape(1, bins))


def faces(gas):
    return call(face_kernel, [shape(240), shape(240), shape(80), shape(1, 1920), shape(1, 1920)], [vmem], 16)(gas)


def make_table(gas):
    return call(table_kernel, shape(blocks * block_rows, dtype=bf16), [vmem], 24)(gas)


unpack_scratch = [
    pltpu.VMEM((bins * 8, lanes), f32), pltpu.VMEM((4, lanes), jnp.int32), pltpu.SMEM((4, lanes), jnp.int32),
]


def sample(received, table):
    return call(
        sample_kernel, jax.ShapeDtypeStruct((peers * 5, 4, lanes), f32), [hbm, vmem], 24,
        [pltpu.VMEM((peers * tiles_out, 4, lanes), f32)] + unpack_scratch
        + [pltpu.VMEM((bins * 40, lanes), f32), pltpu.SemaphoreType.DMA],
    )(received, table)


def deposit(results, received):
    return call(
        deposit_kernel, shape(5 * plane), [vmem, vmem], 24,
        unpack_scratch
        + [pltpu.VMEM((blocks * 40, lanes), f32), pltpu.VMEM((bins * 8, lanes), f32), pltpu.SemaphoreType.DMA],
    )(results, received)


def advance(gas, sources, halos):
    return call(
        flow_kernel, shape(5 * plane), [vmem] * 7, 24,
        [pltpu.VMEM((5 * plane, lanes), f32), pltpu.VMEM((2400, lanes), f32), pltpu.VMEM((80, lanes), f32)],
    )(gas, sources, *halos)


def leave(returned, drops, crossing):
    return call(
        leave_kernel, [shape(bins * 8), shape(8, moving), shape(8, moving)], [vmem, vmem, smem], 16
    )(returned, drops, crossing)


def stay(updated, bin_counts, crossing):
    return call(stay_kernel, shape(bins * 8), [vmem, smem, vmem], 16)(updated, bin_counts, crossing)


def per_device(gas_state, droplets, bin_blocks, bin_counts, crossing):
    gas = gas_state.reshape(5 * plane, lanes)
    drops = droplets.reshape(8, bins, lanes).transpose(1, 0, 2).reshape(bins * 8, lanes)
    received = exchange(pack(drops, bin_blocks, bin_counts))

    x_low, x_high, z_both, y_low, y_high = faces(gas)
    halos = (
        shifted_by(x_high, "gx", 1),
        shifted_by(x_low, "gx", -1),
        shifted_by(z_both, "grp", 1),
        shifted_by(y_high, "gy", 1),
        shifted_by(y_low, "gy", -1),
    )
    table = make_table(gas)
    received, halos = lax.optimization_barrier((received, halos))
    results = sample(received, table)
    returned = exchange(results)
    gas_next = advance(gas, deposit(results, received), halos)
    returned, gas_next = lax.optimization_barrier((returned, gas_next))
    updated, toward_next, toward_previous = leave(returned, drops, crossing)
    from_previous = shifted_by(toward_next, "gx", 1)
    from_next = shifted_by(toward_previous, "gx", -1)
    arrivals = jnp.stack([from_previous, from_next], axis=1)
    kept = stay(updated, bin_counts, crossing)
    droplets_next = kept.reshape(bins, 8, lanes).transpose(1, 0, 2).reshape(8, bins * lanes)
    return gas_next.reshape(gas_state.shape), droplets_next, arrivals


def solution(mesh):
    whole = ("grp", "gx", "gy")
    in_specs = (P(None, "gx", "grp", "gy"), P(None, whole), P(whole), P(whole), P(None, whole))
    out_specs = (P(None, "gx", "grp", "gy"), P(None, whole), P(None, None, whole))
    return jax.shard_map(per_device, mesh=mesh, in_specs=in_specs, out_specs=out_specs, check_vma=False)
```

```python
import jax
import jax.numpy as jnp
from jax import lax
from jax.experimental import pallas as pl
from jax.experimental.pallas import tpu as pltpu
from jax.sharding import PartitionSpec as P

f32 = jnp.float32
bf16 = jnp.bfloat16

peers = 32
per_peer = 4
bins = 128
lanes = 128
blocks = 96
depth, across, height = 8, 48, 128
plane = depth * across
tiles_out = per_peer * 2 + 1
moving = 256
together = 64
per_batch = 64
quarters = 4

vmem = pl.BlockSpec(memory_space=pltpu.VMEM)
smem = pl.BlockSpec(memory_space=pltpu.SMEM)
hbm = pl.BlockSpec(memory_space=pltpu.HBM)


def params(mib):
    return pltpu.CompilerParams(vmem_limit_bytes=mib * 1024 * 1024)


def lane_index(rows):
    return lax.broadcasted_iota(jnp.int32, (rows, lanes), 1)


def split(x):
    high = x.astype(bf16)
    return high, (x - high.astype(f32)).astype(bf16)


def pack_kernel(drops, ids, counts, out, held, numbers, sems):
    copies = [
        pltpu.make_async_copy(drops, held, sems.at[0]),
        pltpu.make_async_copy(ids, numbers.at[0], sems.at[1]),
        pltpu.make_async_copy(counts, numbers.at[1], sems.at[2]),
    ]
    for copy in copies:
        copy.start()
    row = lax.broadcasted_iota(jnp.int32, (4, lanes), 0)
    lane = lane_index(4)
    copies[1].wait()
    copies[2].wait()
    both = jnp.where(row == 0, numbers[0], jnp.where(row == 1, numbers[1], 0)).astype(f32)
    for p in range(peers):
        near = pltpu.roll(both, (lanes - p * per_peer) % lanes, 1) if p else both
        out[p * tiles_out + 8] = jnp.where(lane < per_peer, near, 0.0)
    copies[0].wait()
    for p in range(peers):
        for t in range(8):
            out[p * tiles_out + t] = held[p * 32 + t * 4 : p * 32 + t * 4 + 4, :]


def unpack(held, drops, index, index_smem, sem):
    total = held[8]
    for p in range(1, peers):
        total = total + pltpu.roll(held[p * tiles_out + 8], p * per_peer, 1)
    index[...] = total.astype(jnp.int32)
    copy = pltpu.make_async_copy(index, index_smem, sem)
    copy.start()
    for p in range(peers):
        for t in range(8):
            drops[p * 32 + t * 4 : p * 32 + t * 4 + 4, :] = held[p * tiles_out + t]
    copy.wait()


def face_kernel(gas, crossing, counts, x_low, x_high, z_both, y_low, y_high, keep):
    for v in range(5):
        x_low[v * across : (v + 1) * across, :] = gas[v * plane : v * plane + across, :]
        x_high[v * across : (v + 1) * across, :] = gas[(v + 1) * plane - across : (v + 1) * plane, :]
        z_both[v * 8 : (v + 1) * 8, :] = gas[pl.ds(v * plane, 8, stride=across), :]
        z_both[40 + v * 8 : 40 + (v + 1) * 8, :] = gas[pl.ds(v * plane + across - 1, 8, stride=across), :]
    row = lax.broadcasted_iota(jnp.int32, (8, lanes), 0)
    lane = lane_index(8)
    pick = jnp.where((row == 0) & (lane == 0) | (row == 1) & (lane == lanes - 1), 1.0, 0.0).astype(f32)
    ends = lax.dot_general(
        pick, gas[...], (((1,), (1,)), ((), ())),
        precision=lax.Precision.HIGHEST, preferred_element_type=f32,
    )
    y_low[...] = ends[0:1]
    y_high[...] = ends[1:2]
    row = lax.broadcasted_iota(jnp.int32, (bins, moving), 0)
    departed = None
    for side in range(2):
        slots = crossing[side : side + 1, :]
        in_bin = jnp.where(row == (slots >> 7), 1.0, 0.0).astype(bf16)
        in_lane = jnp.where(row == (slots & (lanes - 1)), 1.0, 0.0).astype(bf16)
        part = lax.dot_general(in_bin, in_lane, (((1,), (1,)), ((), ())), preferred_element_type=f32)
        departed = part if departed is None else departed + part
    lane = lane_index(bins)
    own = lax.broadcasted_iota(jnp.int32, (bins, lanes), 0) == lane
    count = jnp.sum(jnp.where(own, counts[...].astype(f32), 0.0), axis=1, keepdims=True)
    keep[...] = jnp.where(lane.astype(f32) < count, 1.0 - departed, 0.0)


def trade_chunks(tiles, chunk):
    for bit in (1, 2, 4):
        upper = (chunk & bit) != 0
        traded = list(tiles)
        for a in range(8):
            if not a & bit:
                b = a | bit
                traded[a] = jnp.where(upper, pltpu.roll(tiles[b], bit * 8, 1), tiles[a])
                traded[b] = jnp.where(upper, tiles[b], pltpu.roll(tiles[a], lanes - bit * 8, 1))
        tiles = traded
    return tiles


def split_rows(tiles):
    first_high, first_low = split(jnp.concatenate(tiles[0:2], axis=0))
    second_high, second_low = split(jnp.concatenate(tiles[2:4], axis=0))
    last = tiles[4].astype(bf16).astype(f32)
    middle = jnp.concatenate([last, tiles[4] - last], axis=0).astype(bf16)
    return [first_high, second_high, middle, first_low, second_low]


high_rows = (0, 8, 16, 24, 32)
low_rows = (48, 56, 64, 72, 40)
block_rows = 80


def table_kernel(gas, out):
    lane = lane_index(8)
    chunk = lane >> 3
    first = lane < 64

    def strip(bz, carry):
        pairs = []
        for v in range(5):
            layers = [gas[pl.ds(v * plane + bz * 8 + j, 8, stride=across), :] for j in range(8)]
            pairs.append(trade_chunks(layers, chunk))
        for by in range(8):
            here = [pairs[v][by] for v in range(5)]
            other = [pltpu.roll(x, 64, 1) for x in here]
            near = [jnp.where(first, a, b) for a, b in zip(here, other)]
            far = [jnp.where(first, b, a) for a, b in zip(here, other)]
            for number, block in ((by, near), (by + 8, far)):
                start = (bz * 16 + number) * block_rows
                for n, part in enumerate(split_rows(block)):
                    out[pl.ds(pl.multiple_of(start + n * 16, 16), 16), :] = part
        return carry

    lax.fori_loop(0, 6, strip, 0)


def hats(tile):
    node = lax.broadcasted_iota(jnp.int32, (8, lanes), 0).astype(f32)
    return [jnp.maximum(0.0, 1.0 - jnp.abs(tile[a : a + 1] - node)) for a in range(3)]


def pair_weights(hat_z, hat_y):
    high, low = split(jnp.concatenate([hat_z[j : j + 1] * hat_y for j in range(8)], axis=0))
    return jnp.concatenate([high, low], axis=0)


def sample_kernel(received, table, results, drops, index, index_smem, products, sem):
    unpack(received, drops, index, index_smem, sem)

    def some_bins(n, carry):
        for e in range(together):
            b = n * together + e
            hat_x, hat_z, hat_y = hats(drops[pl.ds(pl.multiple_of(b * 8, 8), 8), :])
            rows = table[pl.ds(pl.multiple_of(index_smem[0, b] * block_rows, 16), block_rows), :]
            product = jnp.dot(rows, pair_weights(hat_z, hat_y), preferred_element_type=f32)
            for v in range(5):
                h, l = high_rows[v], low_rows[v]
                products[pl.ds(pl.multiple_of(b * 40 + v * 8, 8), 8), :] = (product[h : h + 8] + product[l : l + 8]) * hat_x
        return carry

    lax.fori_loop(0, bins // together, some_bins, 0)

    def some_groups(n, carry):
        for e in range(4):
            g = n * 4 + e
            sampled = []
            for v in range(5):
                terms = [products[pl.ds(g * 320 + v * 8 + i, 8, stride=40), :] for i in range(8)]
                while len(terms) > 1:
                    terms = [a + b for a, b in zip(terms[0::2], terms[1::2])]
                sampled.append(terms[0])
            density, m1, m2, m3, energy = sampled
            v1, v2, v3, mass, heat = [drops[pl.ds(g * 64 + v, 8, stride=8), :] for v in range(3, 8)]
            inverse = 1.0 / density
            u1, u2, u3 = m1 * inverse, m2 * inverse, m3 * inverse
            gas_heat = 0.4 * (energy - 0.5 * (m1 * u1 + m2 * u2 + m3 * u3)) * inverse
            inverse_area = jnp.exp(jnp.log(mass) * (-2.0 / 3.0))
            rate = density * inverse_area * -0.8
            drag = jnp.exp(rate)
            values = [
                u1 + (v1 - u1) * drag,
                u2 + (v2 - u2) * drag,
                u3 + (v3 - u3) * drag,
                mass * jnp.exp(-0.2 * gas_heat * heat * inverse_area),
                gas_heat + (heat - gas_heat) * jnp.exp(rate * (1.0 / 1.5)),
            ]
            for v in range(5):
                results[g * 10 + v] = values[v][0:4]
                results[g * 10 + 5 + v] = values[v][4:8]
        return carry

    lax.fori_loop(0, 4, some_groups, 0)


def group_values(results, g):
    return [jnp.concatenate([results[g * 10 + v], results[g * 10 + 5 + v]], axis=0) for v in range(5)]


def primitives(s):
    inverse = 1.0 / s[0]
    u = [s[1] * inverse, s[2] * inverse, s[3] * inverse]
    pressure = 0.4 * (s[4] - 0.5 * (s[1] * u[0] + s[2] * u[1] + s[3] * u[2]))
    return u, pressure


def flux(s, u, pressure, a):
    normal = u[a]
    out = [s[1 + a]]
    for c in range(3):
        out.append(s[1 + c] * normal + pressure if c == a else s[1 + c] * normal)
    out.append((s[4] + pressure) * normal)
    return out


def deposit_kernel(results, received, out, drops, index, index_smem, sums, gains, sem):
    sums[...] = jnp.zeros(sums.shape, f32)
    unpack(received, drops, index, index_smem, sem)

    def some_groups(n, carry):
        for e in range(4):
            g = n * 4 + e
            v1, v2, v3, mass, heat = [drops[pl.ds(g * 64 + v, 8, stride=8), :] for v in range(3, 8)]
            w1, w2, w3, mass_new, heat_new = group_values(results, g)
            values = [
                mass - mass_new,
                mass * v1 - mass_new * w1,
                mass * v2 - mass_new * w2,
                mass * v3 - mass_new * w3,
                0.5 * mass * (v1 * v1 + v2 * v2 + v3 * v3) + mass * heat
                - 0.5 * mass_new * (w1 * w1 + w2 * w2 + w3 * w3) - mass_new * heat_new,
            ]
            for v in range(5):
                gains[pl.ds(g * 64 + v, 8, stride=8), :] = 4.0 * values[v]
        return carry

    lax.fori_loop(0, 4, some_groups, 0)
    lane8 = lane_index(8)

    def some_bins(n, carry):
        for e in range(together):
            b = n * together + e
            here = pl.ds(pl.multiple_of(b * 8, 8), 8)
            hat_x, hat_z, hat_y = hats(drops[here, :])
            live = jnp.where(lane8 < index_smem[1, b], gains[here, :], 0.0)
            spread = jnp.concatenate(split_rows([live[v : v + 1] * hat_x for v in range(5)]), axis=0)
            added = lax.dot_general(
                spread, pair_weights(hat_z, hat_y), (((1,), (1,)), ((), ())), preferred_element_type=f32
            )
            start = index_smem[0, b] * 40
            for v in range(5):
                h, l = high_rows[v], low_rows[v]
                place = pl.ds(pl.multiple_of(start + v * 8, 8), 8)
                sums[place, :] = sums[place, :] + (added[h : h + 8] + added[l : l + 8])
        return carry

    lax.fori_loop(0, bins // together, some_bins, 0)
    chunk = lane8 >> 3
    first = lane8 < 64

    def strip(bz, carry):
        for v in range(5):
            pairs = []
            for by in range(8):
                near = sums[pl.ds(pl.multiple_of((bz * 16 + by) * 40 + v * 8, 8), 8), :]
                far = sums[pl.ds(pl.multiple_of((bz * 16 + by + 8) * 40 + v * 8, 8), 8), :]
                pairs.append(jnp.where(first, near + pltpu.roll(near, 64, 1), far + pltpu.roll(far, 64, 1)))
            for j, layer in enumerate(trade_chunks(pairs, chunk)):
                out[pl.ds(v * plane + bz * 8 + j, 8, stride=across), :] = layer
        return carry

    lax.fori_loop(0, 6, strip, 0)


def flow_kernel(gas, sources, x_low, x_high, z_both, y_low, y_high, out, y_ends, x_padded, z_flux):
    row8 = lax.broadcasted_iota(jnp.int32, (8, lanes), 0)
    lane8 = lane_index(8)
    place = jnp.where((row8 == 0) & (lane8 == 0) | (row8 == 1) & (lane8 == lanes - 1), 1.0, 0.0).astype(f32)
    ends = jnp.concatenate([y_low[...], y_high[...], jnp.zeros((6, 5 * plane), f32)], axis=0)
    y_ends[...] = lax.dot_general(
        ends, place, (((0,), (0,)), ((), ())),
        precision=lax.Precision.HIGHEST, preferred_element_type=f32,
    )
    for v in range(5):
        x_padded[v * 480 : v * 480 + across, :] = x_low[v * across : (v + 1) * across, :]
        x_padded[v * 480 + across : v * 480 + 432, :] = gas[v * plane : (v + 1) * plane, :]
        x_padded[v * 480 + 432 : (v + 1) * 480, :] = x_high[v * across : (v + 1) * across, :]
    for side in range(2):
        edge = [z_both[side * 40 + v * 8 : side * 40 + (v + 1) * 8, :] for v in range(5)]
        edge_flux = flux(edge, *primitives(edge), 1)
        for v in range(5):
            z_flux[side * 40 + v * 8 : side * 40 + (v + 1) * 8, :] = edge_flux[v]

    row = lax.broadcasted_iota(jnp.int32, (across, lanes), 0)
    lane = lane_index(across)

    def layer(i, carry):
        def cells(at):
            return [x_padded[pl.ds(pl.multiple_of(v * 480 + at * across, 8), across), :] for v in range(5)]

        def rows(v):
            return pl.ds(pl.multiple_of(v * plane + i * across, 8), across)

        here, below, above = cells(i + 1), cells(i), cells(i + 2)
        u, pressure = primitives(here)
        flux_above = flux(above, *primitives(above), 0)
        flux_below = flux(below, *primitives(below), 0)
        flux_z = flux(here, u, pressure, 1)
        flux_y = flux(here, u, pressure, 2)
        ends = [y_ends[rows(v), :] for v in range(5)]
        flux_ends = flux(ends, *primitives(ends), 2)
        for v in range(5):
            z_low = z_both[pl.ds(40 + v * 8 + i, 1), :]
            z_high = z_both[pl.ds(v * 8 + i, 1), :]
            z_low_flux = z_flux[pl.ds(40 + v * 8 + i, 1), :]
            z_high_flux = z_flux[pl.ds(v * 8 + i, 1), :]

            def z_pair(x, low, high):
                return (
                    jnp.where(row == 0, low, pltpu.roll(x, 1, 0)),
                    jnp.where(row == across - 1, high, pltpu.roll(x, across - 1, 0)),
                )

            def y_pair(x, end):
                return (
                    jnp.where(lane == 0, end, pltpu.roll(x, 1, 1)),
                    jnp.where(lane == lanes - 1, end, pltpu.roll(x, lanes - 1, 1)),
                )

            z_down, z_up = z_pair(here[v], z_low, z_high)
            z_flux_down, z_flux_up = z_pair(flux_z[v], z_low_flux, z_high_flux)
            y_down, y_up = y_pair(here[v], ends[v])
            y_flux_down, y_flux_up = y_pair(flux_y[v], flux_ends[v])
            spread = (below[v] + above[v]) + (z_down + z_up) + (y_down + y_up) - 6.0 * here[v]
            change = (flux_above[v] - flux_below[v]) + (z_flux_up - z_flux_down) + (y_flux_up - y_flux_down)
            flow = 0.5 * change - 1.5 * spread
            out[rows(v), :] = here[v] - 0.1 * flow + sources[rows(v), :]
        return carry

    lax.fori_loop(0, depth, layer, 0)


def leave_kernel(returned, drops, keep, crossing, stay, toward_next, toward_previous, updated, staying, sems):
    copies = []
    for g in range(bins // 8):
        values = group_values(returned, g)
        places = [drops[pl.ds(g * 64 + a, 8, stride=8), :] + 0.2 * values[a] for a in range(3)]
        mask = keep[g * 8 : (g + 1) * 8, :]
        for n, value in enumerate(places + values):
            at = pl.ds(g * 64 + n, 8, stride=8)
            updated[at, :] = value
            staying[at, :] = value * mask
        if g % 4 == 3:
            part = pl.ds((g - 3) * 64, 256)
            copies.append(pltpu.make_async_copy(staying.at[part], stay.at[part], sems.at[g // 4]))
            copies[-1].start()

    lane = lane_index(8)

    def batch(s, carry):
        tiles = list(carry)
        for e in range(per_batch):
            for t in range(4):
                target = s * per_batch + e
                slot = crossing[t // 2, (t % 2) * lanes + target]
                tile = updated[pl.ds(pl.multiple_of((slot >> 7) * 8, 8), 8), :]
                moved = pltpu.roll(tile, (target - slot) & (lanes - 1), 1)
                tiles[t] = jnp.where(lane == target, moved, tiles[t])
        return tuple(tiles)

    tiles = lax.fori_loop(0, lanes // per_batch, batch, (jnp.zeros((8, lanes), f32),) * 4)
    toward_next[...] = jnp.concatenate(tiles[0:2], axis=1)
    toward_previous[...] = jnp.concatenate(tiles[2:4], axis=1)
    for copy in copies:
        copy.wait()


def shape(rows, columns=lanes, dtype=f32):
    return jax.ShapeDtypeStruct((rows, columns), dtype)


def shifted_by(x, axis, by):
    count = lax.axis_size(axis)
    return lax.ppermute(x, axis, [(i, (i + by) % count) for i in range(count)])


def exchange(x):
    return lax.all_to_all(x, "gx", split_axis=0, concat_axis=0, tiled=True)


def call(kernel, out_shape, in_specs, mib, scratch=(), out_specs=None):
    if out_specs is None:
        out_specs = [vmem] * len(out_shape) if isinstance(out_shape, list) else vmem
    return pl.pallas_call(
        kernel, name=kernel.__name__, out_shape=out_shape, in_specs=in_specs,
        out_specs=out_specs, scratch_shapes=list(scratch), compiler_params=params(mib),
    )


def pack(drops, bin_blocks, bin_counts):
    return call(
        pack_kernel, jax.ShapeDtypeStruct((peers * tiles_out, 4, lanes), f32), [hbm] * 3, 60,
        [pltpu.VMEM((bins * 8, lanes), f32), pltpu.VMEM((2, 1, lanes), jnp.int32), pltpu.SemaphoreType.DMA((3,))],
    )(drops, bin_blocks.reshape(1, bins), bin_counts.reshape(1, bins))


def faces(gas, crossing, bin_counts):
    return call(
        face_kernel,
        [shape(240), shape(240), shape(80), shape(1, 1920), shape(1, 1920), shape(bins)], [vmem] * 3, 16,
    )(gas, crossing, bin_counts.reshape(1, bins))


def make_table(gas):
    return call(table_kernel, shape(blocks * block_rows, dtype=bf16), [vmem], 24)(gas)


unpack_scratch = [
    pltpu.VMEM((bins * 8, lanes), f32), pltpu.VMEM((4, lanes), jnp.int32), pltpu.SMEM((4, lanes), jnp.int32),
]


def sample(received, table):
    return call(
        sample_kernel, jax.ShapeDtypeStruct((peers * 5, 4, lanes), f32), [vmem] * 2, 24,
        unpack_scratch + [pltpu.VMEM((bins * 40, lanes), f32), pltpu.SemaphoreType.DMA],
    )(received, table)


def deposit(results, received):
    return call(
        deposit_kernel, shape(5 * plane), [vmem, vmem], 24,
        unpack_scratch
        + [pltpu.VMEM((blocks * 40, lanes), f32), pltpu.VMEM((bins * 8, lanes), f32), pltpu.SemaphoreType.DMA],
    )(results, received)


def advance(gas, sources, halos):
    return call(
        flow_kernel, shape(5 * plane), [vmem] * 7, 24,
        [pltpu.VMEM((5 * plane, lanes), f32), pltpu.VMEM((2400, lanes), f32), pltpu.VMEM((80, lanes), f32)],
    )(gas, sources, *halos)


def leave(returned, drops, keep, crossing):
    return call(
        leave_kernel, [shape(bins * 8), shape(8, moving), shape(8, moving)], [vmem] * 3 + [smem], 16,
        [pltpu.VMEM((bins * 8, lanes), f32), pltpu.VMEM((bins * 8, lanes), f32), pltpu.SemaphoreType.DMA((4,))],
        [hbm, vmem, vmem],
    )(returned, drops, keep, crossing)


def per_device(gas_state, droplets, bin_blocks, bin_counts, crossing):
    gas = gas_state.reshape(5 * plane, lanes)
    drops = droplets.reshape(8, bins, lanes).transpose(1, 0, 2).reshape(bins * 8, lanes)
    received = exchange(pack(drops, bin_blocks, bin_counts))

    x_low, x_high, z_both, y_low, y_high, keep = faces(gas, crossing, bin_counts)
    halos = (
        shifted_by(x_high, "gx", 1),
        shifted_by(x_low, "gx", -1),
        shifted_by(z_both, "grp", 1),
        shifted_by(y_high, "gy", 1),
        shifted_by(y_low, "gy", -1),
    )
    table = make_table(gas)
    received, halos_z, halos_y1, halos_y2 = lax.optimization_barrier((received,) + halos[2:])
    results = sample(received, table)
    results, halo_x1, halo_x2 = lax.optimization_barrier((results,) + halos[:2])
    halos = (halo_x1, halo_x2, halos_z, halos_y1, halos_y2)
    returned = exchange(results)
    gas_next = advance(gas, deposit(results, received), halos)
    returned, gas_next = lax.optimization_barrier((returned, gas_next))
    kept, toward_next, toward_previous = leave(returned, drops, keep, crossing)
    from_previous = shifted_by(toward_next, "gx", 1)
    from_next = shifted_by(toward_previous, "gx", -1)
    arrivals = jnp.stack([from_previous, from_next], axis=1)
    droplets_next = kept.reshape(bins, 8, lanes).transpose(1, 0, 2).reshape(8, bins * lanes)
    return gas_next.reshape(gas_state.shape), droplets_next, arrivals


def solution(mesh):
    whole = ("grp", "gx", "gy")
    in_specs = (P(None, "gx", "grp", "gy"), P(None, whole), P(whole), P(whole), P(None, whole))
    out_specs = (P(None, "gx", "grp", "gy"), P(None, whole), P(None, None, whole))
    return jax.shard_map(per_device, mesh=mesh, in_specs=in_specs, out_specs=out_specs, check_vma=False)
```

```python
import jax
import jax.numpy as jnp
from jax import lax
from jax.experimental import pallas as pl
from jax.experimental.pallas import tpu as pltpu
from jax.sharding import PartitionSpec as P

f32 = jnp.float32
bf16 = jnp.bfloat16

peers = 32
per_peer = 4
bins = 128
lanes = 128
blocks = 96
depth, across, height = 8, 48, 128
plane = depth * across
tiles_out = per_peer * 2 + 1
moving = 256
together = 64
per_batch = 64
quarters = 4

vmem = pl.BlockSpec(memory_space=pltpu.VMEM)
smem = pl.BlockSpec(memory_space=pltpu.SMEM)
hbm = pl.BlockSpec(memory_space=pltpu.HBM)


def params(mib):
    return pltpu.CompilerParams(vmem_limit_bytes=mib * 1024 * 1024)


def lane_index(rows):
    return lax.broadcasted_iota(jnp.int32, (rows, lanes), 1)


def split(x):
    high = x.astype(bf16)
    return high, (x - high.astype(f32)).astype(bf16)


def pack_kernel(drops, ids, counts, out, held, numbers, sems):
    copies = [
        pltpu.make_async_copy(drops, held, sems.at[0]),
        pltpu.make_async_copy(ids, numbers.at[0], sems.at[1]),
        pltpu.make_async_copy(counts, numbers.at[1], sems.at[2]),
    ]
    for copy in copies:
        copy.start()
    row = lax.broadcasted_iota(jnp.int32, (4, lanes), 0)
    lane = lane_index(4)
    copies[1].wait()
    copies[2].wait()
    both = jnp.where(row == 0, numbers[0], jnp.where(row == 1, numbers[1], 0)).astype(f32)
    for p in range(peers):
        near = pltpu.roll(both, (lanes - p * per_peer) % lanes, 1) if p else both
        out[p * tiles_out + 8] = jnp.where(lane < per_peer, near, 0.0)
    copies[0].wait()
    for p in range(peers):
        for t in range(8):
            out[p * tiles_out + t] = held[p * 32 + t * 4 : p * 32 + t * 4 + 4, :]


def unpack(held, drops, index, index_smem, sem):
    total = held[8]
    for p in range(1, peers):
        total = total + pltpu.roll(held[p * tiles_out + 8], p * per_peer, 1)
    index[...] = total.astype(jnp.int32)
    copy = pltpu.make_async_copy(index, index_smem, sem)
    copy.start()
    for p in range(peers):
        for t in range(8):
            drops[p * 32 + t * 4 : p * 32 + t * 4 + 4, :] = held[p * tiles_out + t]
    return copy


def face_kernel(gas, crossing, counts, x_low, x_high, z_both, y_low, y_high, keep):
    for v in range(5):
        x_low[v * across : (v + 1) * across, :] = gas[v * plane : v * plane + across, :]
        x_high[v * across : (v + 1) * across, :] = gas[(v + 1) * plane - across : (v + 1) * plane, :]
        z_both[v * 8 : (v + 1) * 8, :] = gas[pl.ds(v * plane, 8, stride=across), :]
        z_both[40 + v * 8 : 40 + (v + 1) * 8, :] = gas[pl.ds(v * plane + across - 1, 8, stride=across), :]
    row = lax.broadcasted_iota(jnp.int32, (8, lanes), 0)
    lane = lane_index(8)
    pick = jnp.where((row == 0) & (lane == 0) | (row == 1) & (lane == lanes - 1), 1.0, 0.0).astype(f32)
    ends = lax.dot_general(
        pick, gas[...], (((1,), (1,)), ((), ())),
        precision=lax.Precision.HIGHEST, preferred_element_type=f32,
    )
    y_low[...] = ends[0:1]
    y_high[...] = ends[1:2]
    row = lax.broadcasted_iota(jnp.int32, (bins, moving), 0)
    departed = None
    for side in range(2):
        slots = crossing[side : side + 1, :]
        in_bin = jnp.where(row == (slots >> 7), 1.0, 0.0).astype(bf16)
        in_lane = jnp.where(row == (slots & (lanes - 1)), 1.0, 0.0).astype(bf16)
        part = lax.dot_general(in_bin, in_lane, (((1,), (1,)), ((), ())), preferred_element_type=f32)
        departed = part if departed is None else departed + part
    lane = lane_index(bins)
    own = lax.broadcasted_iota(jnp.int32, (bins, lanes), 0) == lane
    count = jnp.sum(jnp.where(own, counts[...].astype(f32), 0.0), axis=1, keepdims=True)
    keep[...] = jnp.where(lane.astype(f32) < count, 1.0 - departed, 0.0)


def trade_chunks(tiles, chunk):
    for bit in (1, 2, 4):
        upper = (chunk & bit) != 0
        traded = list(tiles)
        for a in range(8):
            if not a & bit:
                b = a | bit
                traded[a] = jnp.where(upper, pltpu.roll(tiles[b], bit * 8, 1), tiles[a])
                traded[b] = jnp.where(upper, tiles[b], pltpu.roll(tiles[a], lanes - bit * 8, 1))
        tiles = traded
    return tiles


def split_rows(tiles):
    first_high, first_low = split(jnp.concatenate(tiles[0:2], axis=0))
    second_high, second_low = split(jnp.concatenate(tiles[2:4], axis=0))
    last = tiles[4].astype(bf16).astype(f32)
    middle = jnp.concatenate([last, tiles[4] - last], axis=0).astype(bf16)
    return [first_high, second_high, middle, first_low, second_low]


high_rows = (0, 8, 16, 24, 32)
low_rows = (48, 56, 64, 72, 40)
block_rows = 80


def table_kernel(gas, out):
    lane = lane_index(8)
    chunk = lane >> 3
    first = lane < 64

    def strip(bz, carry):
        pairs = []
        for v in range(5):
            layers = [gas[pl.ds(v * plane + bz * 8 + j, 8, stride=across), :] for j in range(8)]
            pairs.append(trade_chunks(layers, chunk))
        for by in range(8):
            here = [pairs[v][by] for v in range(5)]
            other = [pltpu.roll(x, 64, 1) for x in here]
            near = [jnp.where(first, a, b) for a, b in zip(here, other)]
            far = [jnp.where(first, b, a) for a, b in zip(here, other)]
            for number, block in ((by, near), (by + 8, far)):
                start = (bz * 16 + number) * block_rows
                for n, part in enumerate(split_rows(block)):
                    out[pl.ds(pl.multiple_of(start + n * 16, 16), 16), :] = part
        return carry

    lax.fori_loop(0, 6, strip, 0)


def hats(tile):
    node = lax.broadcasted_iota(jnp.int32, (8, lanes), 0).astype(f32)
    return [jnp.maximum(0.0, 1.0 - jnp.abs(tile[a : a + 1] - node)) for a in range(3)]


def pair_weights(hat_z, hat_y):
    high, low = split(jnp.concatenate([hat_z[j : j + 1] * hat_y for j in range(8)], axis=0))
    return jnp.concatenate([high, low], axis=0)


def sample_kernel(received, table, results, drops, index, index_smem, products, answers, sems):
    unpack(received, drops, index, index_smem, sems.at[quarters]).wait()
    stores = []
    for n in range(quarters):
        for b in range(n * 32, n * 32 + 32):
            hat_x, hat_z, hat_y = hats(drops[b * 8 : b * 8 + 8, :])
            rows = table[pl.ds(pl.multiple_of(index_smem[0, b] * block_rows, 16), block_rows), :]
            product = jnp.dot(rows, pair_weights(hat_z, hat_y), preferred_element_type=f32)
            for v in range(5):
                h, l = high_rows[v], low_rows[v]
                at = b * 40 + v * 8
                products[at : at + 8, :] = (product[h : h + 8] + product[l : l + 8]) * hat_x
        for g in range(n * 4, n * 4 + 4):
            sampled = []
            for v in range(5):
                terms = [products[pl.ds(g * 320 + v * 8 + i, 8, stride=40), :] for i in range(8)]
                while len(terms) > 1:
                    terms = [a + b for a, b in zip(terms[0::2], terms[1::2])]
                sampled.append(terms[0])
            density, m1, m2, m3, energy = sampled
            v1, v2, v3, mass, heat = [drops[pl.ds(g * 64 + v, 8, stride=8), :] for v in range(3, 8)]
            inverse = 1.0 / density
            u1, u2, u3 = m1 * inverse, m2 * inverse, m3 * inverse
            gas_heat = 0.4 * (energy - 0.5 * (m1 * u1 + m2 * u2 + m3 * u3)) * inverse
            inverse_area = jnp.exp(jnp.log(mass) * (-2.0 / 3.0))
            rate = density * inverse_area * -0.8
            drag = jnp.exp(rate)
            values = [
                u1 + (v1 - u1) * drag,
                u2 + (v2 - u2) * drag,
                u3 + (v3 - u3) * drag,
                mass * jnp.exp(-0.2 * gas_heat * heat * inverse_area),
                gas_heat + (heat - gas_heat) * jnp.exp(rate * (1.0 / 1.5)),
            ]
            for v in range(5):
                answers[g * 10 + v] = values[v][0:4]
                answers[g * 10 + 5 + v] = values[v][4:8]
        part = pl.ds(n * 40, 40)
        stores.append(pltpu.make_async_copy(answers.at[part], results.at[part], sems.at[n]))
        stores[n].start()
    for copy in stores:
        copy.wait()


def group_values(results, g):
    return [jnp.concatenate([results[g * 10 + v], results[g * 10 + 5 + v]], axis=0) for v in range(5)]


def primitives(s):
    inverse = 1.0 / s[0]
    u = [s[1] * inverse, s[2] * inverse, s[3] * inverse]
    pressure = 0.4 * (s[4] - 0.5 * (s[1] * u[0] + s[2] * u[1] + s[3] * u[2]))
    return u, pressure


def flux(s, u, pressure, a):
    normal = u[a]
    out = [s[1 + a]]
    for c in range(3):
        out.append(s[1 + c] * normal + pressure if c == a else s[1 + c] * normal)
    out.append((s[4] + pressure) * normal)
    return out


def deposit_kernel(results, received, out, answers, drops, index, index_smem, sums, gains, sems):
    load = pltpu.make_async_copy(results, answers, sems.at[1])
    load.start()
    copy = unpack(received, drops, index, index_smem, sems.at[0])
    sums[...] = jnp.zeros(sums.shape, f32)
    load.wait()

    def some_groups(n, carry):
        for e in range(4):
            g = n * 4 + e
            v1, v2, v3, mass, heat = [drops[pl.ds(g * 64 + v, 8, stride=8), :] for v in range(3, 8)]
            w1, w2, w3, mass_new, heat_new = group_values(answers, g)
            values = [
                mass - mass_new,
                mass * v1 - mass_new * w1,
                mass * v2 - mass_new * w2,
                mass * v3 - mass_new * w3,
                0.5 * mass * (v1 * v1 + v2 * v2 + v3 * v3) + mass * heat
                - 0.5 * mass_new * (w1 * w1 + w2 * w2 + w3 * w3) - mass_new * heat_new,
            ]
            for v in range(5):
                gains[pl.ds(g * 64 + v, 8, stride=8), :] = 4.0 * values[v]
        return carry

    lax.fori_loop(0, 4, some_groups, 0)
    copy.wait()
    lane8 = lane_index(8)

    def some_bins(n, carry):
        for e in range(together):
            b = n * together + e
            here = pl.ds(pl.multiple_of(b * 8, 8), 8)
            hat_x, hat_z, hat_y = hats(drops[here, :])
            live = jnp.where(lane8 < index_smem[1, b], gains[here, :], 0.0)
            spread = jnp.concatenate(split_rows([live[v : v + 1] * hat_x for v in range(5)]), axis=0)
            added = lax.dot_general(
                spread, pair_weights(hat_z, hat_y), (((1,), (1,)), ((), ())), preferred_element_type=f32
            )
            start = index_smem[0, b] * 40
            for v in range(5):
                h, l = high_rows[v], low_rows[v]
                place = pl.ds(pl.multiple_of(start + v * 8, 8), 8)
                sums[place, :] = sums[place, :] + (added[h : h + 8] + added[l : l + 8])
        return carry

    lax.fori_loop(0, bins // together, some_bins, 0)
    chunk = lane8 >> 3
    first = lane8 < 64

    def strip(bz, carry):
        for v in range(5):
            pairs = []
            for by in range(8):
                near = sums[pl.ds(pl.multiple_of((bz * 16 + by) * 40 + v * 8, 8), 8), :]
                far = sums[pl.ds(pl.multiple_of((bz * 16 + by + 8) * 40 + v * 8, 8), 8), :]
                pairs.append(jnp.where(first, near + pltpu.roll(near, 64, 1), far + pltpu.roll(far, 64, 1)))
            for j, layer in enumerate(trade_chunks(pairs, chunk)):
                out[pl.ds(v * plane + bz * 8 + j, 8, stride=across), :] = layer
        return carry

    lax.fori_loop(0, 6, strip, 0)


def flow_kernel(gas, sources, x_low, x_high, z_both, y_low, y_high, out, y_ends, x_padded, z_flux):
    row8 = lax.broadcasted_iota(jnp.int32, (8, lanes), 0)
    lane8 = lane_index(8)
    place = jnp.where((row8 == 0) & (lane8 == 0) | (row8 == 1) & (lane8 == lanes - 1), 1.0, 0.0).astype(f32)
    ends = jnp.concatenate([y_low[...], y_high[...], jnp.zeros((6, 5 * plane), f32)], axis=0)
    y_ends[...] = lax.dot_general(
        ends, place, (((0,), (0,)), ((), ())),
        precision=lax.Precision.HIGHEST, preferred_element_type=f32,
    )
    for v in range(5):
        x_padded[v * 480 : v * 480 + across, :] = x_low[v * across : (v + 1) * across, :]
        x_padded[v * 480 + across : v * 480 + 432, :] = gas[v * plane : (v + 1) * plane, :]
        x_padded[v * 480 + 432 : (v + 1) * 480, :] = x_high[v * across : (v + 1) * across, :]
    for side in range(2):
        edge = [z_both[side * 40 + v * 8 : side * 40 + (v + 1) * 8, :] for v in range(5)]
        edge_flux = flux(edge, *primitives(edge), 1)
        for v in range(5):
            z_flux[side * 40 + v * 8 : side * 40 + (v + 1) * 8, :] = edge_flux[v]

    row = lax.broadcasted_iota(jnp.int32, (across, lanes), 0)
    lane = lane_index(across)

    def layer(i, carry):
        def cells(at):
            return [x_padded[pl.ds(pl.multiple_of(v * 480 + at * across, 8), across), :] for v in range(5)]

        def rows(v):
            return pl.ds(pl.multiple_of(v * plane + i * across, 8), across)

        here, below, above = cells(i + 1), cells(i), cells(i + 2)
        u, pressure = primitives(here)
        flux_above = flux(above, *primitives(above), 0)
        flux_below = flux(below, *primitives(below), 0)
        flux_z = flux(here, u, pressure, 1)
        flux_y = flux(here, u, pressure, 2)
        ends = [y_ends[rows(v), :] for v in range(5)]
        flux_ends = flux(ends, *primitives(ends), 2)
        for v in range(5):
            z_low = z_both[pl.ds(40 + v * 8 + i, 1), :]
            z_high = z_both[pl.ds(v * 8 + i, 1), :]
            z_low_flux = z_flux[pl.ds(40 + v * 8 + i, 1), :]
            z_high_flux = z_flux[pl.ds(v * 8 + i, 1), :]

            def z_pair(x, low, high):
                return (
                    jnp.where(row == 0, low, pltpu.roll(x, 1, 0)),
                    jnp.where(row == across - 1, high, pltpu.roll(x, across - 1, 0)),
                )

            def y_pair(x, end):
                return (
                    jnp.where(lane == 0, end, pltpu.roll(x, 1, 1)),
                    jnp.where(lane == lanes - 1, end, pltpu.roll(x, lanes - 1, 1)),
                )

            z_down, z_up = z_pair(here[v], z_low, z_high)
            z_flux_down, z_flux_up = z_pair(flux_z[v], z_low_flux, z_high_flux)
            y_down, y_up = y_pair(here[v], ends[v])
            y_flux_down, y_flux_up = y_pair(flux_y[v], flux_ends[v])
            spread = (below[v] + above[v]) + (z_down + z_up) + (y_down + y_up) - 6.0 * here[v]
            change = (flux_above[v] - flux_below[v]) + (z_flux_up - z_flux_down) + (y_flux_up - y_flux_down)
            flow = 0.5 * change - 1.5 * spread
            out[rows(v), :] = here[v] - 0.1 * flow + sources[rows(v), :]
        return carry

    lax.fori_loop(0, depth, layer, 0)


def leave_kernel(returned, drops, crossing, updated, toward_next, toward_previous, slots, sem):
    copy = pltpu.make_async_copy(crossing, slots, sem)
    copy.start()
    for g in range(bins // 8):
        values = group_values(returned, g)
        places = [drops[pl.ds(g * 64 + a, 8, stride=8), :] + 0.2 * values[a] for a in range(3)]
        for n, value in enumerate(places + values):
            updated[pl.ds(g * 64 + n, 8, stride=8), :] = value
    copy.wait()

    lane = lane_index(8)

    def batch(s, carry):
        tiles = list(carry)
        for e in range(per_batch):
            for t in range(4):
                target = s * per_batch + e
                slot = slots[t // 2, (t % 2) * lanes + target]
                tile = updated[pl.ds(pl.multiple_of((slot >> 7) * 8, 8), 8), :]
                moved = pltpu.roll(tile, (target - slot) & (lanes - 1), 1)
                tiles[t] = jnp.where(lane == target, moved, tiles[t])
        return tuple(tiles)

    tiles = lax.fori_loop(0, lanes // per_batch, batch, (jnp.zeros((8, lanes), f32),) * 4)
    toward_next[...] = jnp.concatenate(tiles[0:2], axis=1)
    toward_previous[...] = jnp.concatenate(tiles[2:4], axis=1)


def stay_kernel(updated, keep, out, staying, sems):
    copies = []
    for n in range(quarters):
        for b in range(n * 32, n * 32 + 32):
            staying[b * 8 : (b + 1) * 8, :] = updated[b * 8 : (b + 1) * 8, :] * keep[b : b + 1, :]
        part = pl.ds(n * 256, 256)
        copies.append(pltpu.make_async_copy(staying.at[part], out.at[part], sems.at[n]))
        copies[n].start()
    for copy in copies:
        copy.wait()


def shape(rows, columns=lanes, dtype=f32):
    return jax.ShapeDtypeStruct((rows, columns), dtype)


def shifted_by(x, axis, by):
    count = lax.axis_size(axis)
    return lax.ppermute(x, axis, [(i, (i + by) % count) for i in range(count)])


def exchange(x):
    return lax.all_to_all(x, "gx", split_axis=0, concat_axis=0, tiled=True)


def call(kernel, out_shape, in_specs, mib, scratch=(), out_specs=None):
    if out_specs is None:
        out_specs = [vmem] * len(out_shape) if isinstance(out_shape, list) else vmem
    return pl.pallas_call(
        kernel, name=kernel.__name__, out_shape=out_shape, in_specs=in_specs,
        out_specs=out_specs, scratch_shapes=list(scratch), compiler_params=params(mib),
    )


def pack(drops, bin_blocks, bin_counts):
    return call(
        pack_kernel, jax.ShapeDtypeStruct((peers * tiles_out, 4, lanes), f32), [hbm] * 3, 60,
        [pltpu.VMEM((bins * 8, lanes), f32), pltpu.VMEM((2, 1, lanes), jnp.int32), pltpu.SemaphoreType.DMA((3,))],
    )(drops, bin_blocks.reshape(1, bins), bin_counts.reshape(1, bins))


def faces(gas, crossing, bin_counts):
    return call(
        face_kernel,
        [shape(240), shape(240), shape(80), shape(1, 1920), shape(1, 1920), shape(bins)], [vmem] * 3, 16,
    )(gas, crossing, bin_counts.reshape(1, bins))


def make_table(gas):
    return call(table_kernel, shape(blocks * block_rows, dtype=bf16), [vmem], 24)(gas)


unpack_scratch = [
    pltpu.VMEM((bins * 8, lanes), f32), pltpu.VMEM((4, lanes), jnp.int32), pltpu.SMEM((4, lanes), jnp.int32),
]


answer_shape = (peers * 5, 4, lanes)


def sample(received, table):
    return call(
        sample_kernel, pltpu.HBM(answer_shape, f32), [vmem] * 2, 24,
        unpack_scratch
        + [pltpu.VMEM((bins * 40, lanes), f32), pltpu.VMEM(answer_shape, f32),
           pltpu.SemaphoreType.DMA((quarters + 1,))],
        hbm,
    )(received, table)


def deposit(results, received):
    return call(
        deposit_kernel, shape(5 * plane), [hbm, vmem], 24,
        [pltpu.VMEM(answer_shape, f32)] + unpack_scratch
        + [pltpu.VMEM((blocks * 40, lanes), f32), pltpu.VMEM((bins * 8, lanes), f32),
           pltpu.SemaphoreType.DMA((2,))],
    )(pltpu.with_memory_space_constraint(results, pltpu.HBM), received)


def advance(gas, sources, halos):
    return call(
        flow_kernel, shape(5 * plane), [vmem] * 7, 24,
        [pltpu.VMEM((5 * plane, lanes), f32), pltpu.VMEM((2400, lanes), f32), pltpu.VMEM((80, lanes), f32)],
    )(gas, sources, *halos)


def leave(returned, drops, crossing):
    return call(
        leave_kernel, [shape(bins * 8), shape(8, moving), shape(8, moving)], [vmem] * 3, 16,
        [pltpu.SMEM((2, moving), jnp.int32), pltpu.SemaphoreType.DMA],
    )(returned, drops, crossing)


def stay(updated, keep):
    return call(
        stay_kernel, shape(bins * 8), [vmem, vmem], 16,
        [pltpu.VMEM((bins * 8, lanes), f32), pltpu.SemaphoreType.DMA((quarters,))], hbm,
    )(updated, keep)


def per_device(gas_state, droplets, bin_blocks, bin_counts, crossing):
    gas = gas_state.reshape(5 * plane, lanes)
    drops = droplets.reshape(8, bins, lanes).transpose(1, 0, 2).reshape(bins * 8, lanes)
    received = exchange(pack(drops, bin_blocks, bin_counts))

    x_low, x_high, z_both, y_low, y_high, keep = faces(gas, crossing, bin_counts)
    halos = (
        shifted_by(x_high, "gx", 1),
        shifted_by(x_low, "gx", -1),
        shifted_by(z_both, "grp", 1),
        shifted_by(y_high, "gy", 1),
        shifted_by(y_low, "gy", -1),
    )
    table = make_table(gas)
    received, halos_z, halos_y1, halos_y2 = lax.optimization_barrier((received,) + halos[2:])
    results = sample(received, table)
    results, halo_x1, halo_x2 = lax.optimization_barrier((results,) + halos[:2])
    halos = (halo_x1, halo_x2, halos_z, halos_y1, halos_y2)
    returned = exchange(results)
    gas_next = advance(gas, deposit(results, received), halos)
    returned, gas_next = lax.optimization_barrier((returned, gas_next))
    updated, toward_next, toward_previous = leave(returned, drops, crossing)
    from_previous = shifted_by(toward_next, "gx", 1)
    from_next = shifted_by(toward_previous, "gx", -1)
    arrivals = jnp.stack([from_previous, from_next], axis=1)
    kept = stay(updated, keep)
    droplets_next = kept.reshape(bins, 8, lanes).transpose(1, 0, 2).reshape(8, bins * lanes)
    return gas_next.reshape(gas_state.shape), droplets_next, arrivals


def solution(mesh):
    whole = ("grp", "gx", "gy")
    in_specs = (P(None, "gx", "grp", "gy"), P(None, whole), P(whole), P(whole), P(None, whole))
    out_specs = (P(None, "gx", "grp", "gy"), P(None, whole), P(None, None, whole))
    return jax.shard_map(per_device, mesh=mesh, in_specs=in_specs, out_specs=out_specs, check_vma=False)
```

```python
import jax
import jax.numpy as jnp
from jax import lax
from jax.experimental import pallas as pl
from jax.experimental.pallas import tpu as pltpu
from jax.sharding import PartitionSpec as P

f32 = jnp.float32
bf16 = jnp.bfloat16

peers = 32
per_peer = 4
bins = 128
lanes = 128
blocks = 96
depth, across, height = 8, 48, 128
plane = depth * across
tiles_out = per_peer * 2 + 1
moving = 256
together = 64
per_batch = 64
quarters = 4

vmem = pl.BlockSpec(memory_space=pltpu.VMEM)
smem = pl.BlockSpec(memory_space=pltpu.SMEM)
hbm = pl.BlockSpec(memory_space=pltpu.HBM)


def params(mib):
    return pltpu.CompilerParams(vmem_limit_bytes=mib * 1024 * 1024)


def lane_index(rows):
    return lax.broadcasted_iota(jnp.int32, (rows, lanes), 1)


def split(x):
    high = x.astype(bf16)
    return high, (x - high.astype(f32)).astype(bf16)


def pack_kernel(drops, ids, counts, out, held, numbers, sems):
    copies = [
        pltpu.make_async_copy(drops, held, sems.at[0]),
        pltpu.make_async_copy(ids, numbers.at[0], sems.at[1]),
        pltpu.make_async_copy(counts, numbers.at[1], sems.at[2]),
    ]
    for copy in copies:
        copy.start()
    row = lax.broadcasted_iota(jnp.int32, (4, lanes), 0)
    lane = lane_index(4)
    copies[1].wait()
    copies[2].wait()
    both = jnp.where(row == 0, numbers[0], jnp.where(row == 1, numbers[1], 0)).astype(f32)
    for p in range(peers):
        near = pltpu.roll(both, (lanes - p * per_peer) % lanes, 1) if p else both
        out[p * tiles_out + 8] = jnp.where(lane < per_peer, near, 0.0)
    copies[0].wait()
    for p in range(peers):
        for t in range(8):
            out[p * tiles_out + t] = held[p * 32 + t * 4 : p * 32 + t * 4 + 4, :]


def unpack(held, drops, index, index_smem, sem):
    total = held[8]
    for p in range(1, peers):
        total = total + pltpu.roll(held[p * tiles_out + 8], p * per_peer, 1)
    index[...] = total.astype(jnp.int32)
    copy = pltpu.make_async_copy(index, index_smem, sem)
    copy.start()
    for p in range(peers):
        for t in range(8):
            drops[p * 32 + t * 4 : p * 32 + t * 4 + 4, :] = held[p * tiles_out + t]
    return copy


def face_kernel(gas, crossing, counts, x_low, x_high, z_both, y_low, y_high, keep):
    for v in range(5):
        x_low[v * across : (v + 1) * across, :] = gas[v * plane : v * plane + across, :]
        x_high[v * across : (v + 1) * across, :] = gas[(v + 1) * plane - across : (v + 1) * plane, :]
        z_both[v * 8 : (v + 1) * 8, :] = gas[pl.ds(v * plane, 8, stride=across), :]
        z_both[40 + v * 8 : 40 + (v + 1) * 8, :] = gas[pl.ds(v * plane + across - 1, 8, stride=across), :]
    row = lax.broadcasted_iota(jnp.int32, (8, lanes), 0)
    lane = lane_index(8)
    pick = jnp.where((row == 0) & (lane == 0) | (row == 1) & (lane == lanes - 1), 1.0, 0.0).astype(f32)
    ends = lax.dot_general(
        pick, gas[...], (((1,), (1,)), ((), ())),
        precision=lax.Precision.HIGHEST, preferred_element_type=f32,
    )
    y_low[...] = ends[0:1]
    y_high[...] = ends[1:2]
    row = lax.broadcasted_iota(jnp.int32, (bins, moving), 0)
    departed = None
    for side in range(2):
        slots = crossing[side : side + 1, :]
        in_bin = jnp.where(row == (slots >> 7), 1.0, 0.0).astype(bf16)
        in_lane = jnp.where(row == (slots & (lanes - 1)), 1.0, 0.0).astype(bf16)
        part = lax.dot_general(in_bin, in_lane, (((1,), (1,)), ((), ())), preferred_element_type=f32)
        departed = part if departed is None else departed + part
    lane = lane_index(bins)
    own = lax.broadcasted_iota(jnp.int32, (bins, lanes), 0) == lane
    count = jnp.sum(jnp.where(own, counts[...].astype(f32), 0.0), axis=1, keepdims=True)
    keep[...] = jnp.where(lane.astype(f32) < count, 1.0 - departed, 0.0)


def trade_chunks(tiles, chunk):
    for bit in (1, 2, 4):
        upper = (chunk & bit) != 0
        traded = list(tiles)
        for a in range(8):
            if not a & bit:
                b = a | bit
                traded[a] = jnp.where(upper, pltpu.roll(tiles[b], bit * 8, 1), tiles[a])
                traded[b] = jnp.where(upper, tiles[b], pltpu.roll(tiles[a], lanes - bit * 8, 1))
        tiles = traded
    return tiles


def split_rows(tiles):
    first_high, first_low = split(jnp.concatenate(tiles[0:2], axis=0))
    second_high, second_low = split(jnp.concatenate(tiles[2:4], axis=0))
    last = tiles[4].astype(bf16).astype(f32)
    middle = jnp.concatenate([last, tiles[4] - last], axis=0).astype(bf16)
    return [first_high, second_high, middle, first_low, second_low]


high_rows = (0, 8, 16, 24, 32)
low_rows = (48, 56, 64, 72, 40)
block_rows = 80


def table_kernel(gas, out):
    lane = lane_index(8)
    chunk = lane >> 3
    first = lane < 64

    def strip(bz, carry):
        pairs = []
        for v in range(5):
            layers = [gas[pl.ds(v * plane + bz * 8 + j, 8, stride=across), :] for j in range(8)]
            pairs.append(trade_chunks(layers, chunk))
        for by in range(8):
            here = [pairs[v][by] for v in range(5)]
            other = [pltpu.roll(x, 64, 1) for x in here]
            near = [jnp.where(first, a, b) for a, b in zip(here, other)]
            far = [jnp.where(first, b, a) for a, b in zip(here, other)]
            for number, block in ((by, near), (by + 8, far)):
                start = (bz * 16 + number) * block_rows
                for n, part in enumerate(split_rows(block)):
                    out[pl.ds(pl.multiple_of(start + n * 16, 16), 16), :] = part
        return carry

    lax.fori_loop(0, 6, strip, 0)


def hats(tile):
    node = lax.broadcasted_iota(jnp.int32, (8, lanes), 0).astype(f32)
    return [jnp.maximum(0.0, 1.0 - jnp.abs(tile[a : a + 1] - node)) for a in range(3)]


def pair_weights(hat_z, hat_y):
    high, low = split(jnp.concatenate([hat_z[j : j + 1] * hat_y for j in range(8)], axis=0))
    return jnp.concatenate([high, low], axis=0)


def sample_kernel(received, table, results, drops, index, index_smem, products, answers, sems):
    unpack(received, drops, index, index_smem, sems.at[quarters]).wait()
    stores = []
    for n in range(quarters):
        for b in range(n * 32, n * 32 + 32):
            hat_x, hat_z, hat_y = hats(drops[b * 8 : b * 8 + 8, :])
            rows = table[pl.ds(pl.multiple_of(index_smem[0, b] * block_rows, 16), block_rows), :]
            product = jnp.dot(rows, pair_weights(hat_z, hat_y), preferred_element_type=f32)
            for v in range(5):
                h, l = high_rows[v], low_rows[v]
                at = b * 40 + v * 8
                products[at : at + 8, :] = (product[h : h + 8] + product[l : l + 8]) * hat_x
        for g in range(n * 4, n * 4 + 4):
            sampled = []
            for v in range(5):
                terms = [products[pl.ds(g * 320 + v * 8 + i, 8, stride=40), :] for i in range(8)]
                while len(terms) > 1:
                    terms = [a + b for a, b in zip(terms[0::2], terms[1::2])]
                sampled.append(terms[0])
            density, m1, m2, m3, energy = sampled
            v1, v2, v3, mass, heat = [drops[pl.ds(g * 64 + v, 8, stride=8), :] for v in range(3, 8)]
            inverse = 1.0 / density
            u1, u2, u3 = m1 * inverse, m2 * inverse, m3 * inverse
            gas_heat = 0.4 * (energy - 0.5 * (m1 * u1 + m2 * u2 + m3 * u3)) * inverse
            inverse_area = jnp.exp(jnp.log(mass) * (-2.0 / 3.0))
            rate = density * inverse_area * -0.8
            drag = jnp.exp(rate)
            values = [
                u1 + (v1 - u1) * drag,
                u2 + (v2 - u2) * drag,
                u3 + (v3 - u3) * drag,
                mass * jnp.exp(-0.2 * gas_heat * heat * inverse_area),
                gas_heat + (heat - gas_heat) * jnp.exp(rate * (1.0 / 1.5)),
            ]
            for v in range(5):
                answers[g * 10 + v] = values[v][0:4]
                answers[g * 10 + 5 + v] = values[v][4:8]
        part = pl.ds(n * 40, 40)
        stores.append(pltpu.make_async_copy(answers.at[part], results.at[part], sems.at[n]))
        stores[n].start()
    for copy in stores:
        copy.wait()


def group_values(results, g):
    return [jnp.concatenate([results[g * 10 + v], results[g * 10 + 5 + v]], axis=0) for v in range(5)]


def primitives(s):
    inverse = 1.0 / s[0]
    u = [s[1] * inverse, s[2] * inverse, s[3] * inverse]
    pressure = 0.4 * (s[4] - 0.5 * (s[1] * u[0] + s[2] * u[1] + s[3] * u[2]))
    return u, pressure


def flux(s, u, pressure, a):
    normal = u[a]
    out = [s[1 + a]]
    for c in range(3):
        out.append(s[1 + c] * normal + pressure if c == a else s[1 + c] * normal)
    out.append((s[4] + pressure) * normal)
    return out


def deposit_kernel(results, received, out, answers, drops, index, index_smem, sums, gains, sems):
    load = pltpu.make_async_copy(results, answers, sems.at[1])
    load.start()
    copy = unpack(received, drops, index, index_smem, sems.at[0])
    sums[...] = jnp.zeros(sums.shape, f32)
    load.wait()

    def some_groups(n, carry):
        for e in range(4):
            g = n * 4 + e
            v1, v2, v3, mass, heat = [drops[pl.ds(g * 64 + v, 8, stride=8), :] for v in range(3, 8)]
            w1, w2, w3, mass_new, heat_new = group_values(answers, g)
            values = [
                mass - mass_new,
                mass * v1 - mass_new * w1,
                mass * v2 - mass_new * w2,
                mass * v3 - mass_new * w3,
                0.5 * mass * (v1 * v1 + v2 * v2 + v3 * v3) + mass * heat
                - 0.5 * mass_new * (w1 * w1 + w2 * w2 + w3 * w3) - mass_new * heat_new,
            ]
            for v in range(5):
                gains[pl.ds(g * 64 + v, 8, stride=8), :] = 4.0 * values[v]
        return carry

    lax.fori_loop(0, 4, some_groups, 0)
    copy.wait()
    lane8 = lane_index(8)

    def some_bins(n, carry):
        for e in range(together):
            b = n * together + e
            here = pl.ds(pl.multiple_of(b * 8, 8), 8)
            hat_x, hat_z, hat_y = hats(drops[here, :])
            live = jnp.where(lane8 < index_smem[1, b], gains[here, :], 0.0)
            spread = jnp.concatenate(split_rows([live[v : v + 1] * hat_x for v in range(5)]), axis=0)
            added = lax.dot_general(
                spread, pair_weights(hat_z, hat_y), (((1,), (1,)), ((), ())), preferred_element_type=f32
            )
            start = index_smem[0, b] * 40
            for v in range(5):
                h, l = high_rows[v], low_rows[v]
                place = pl.ds(pl.multiple_of(start + v * 8, 8), 8)
                sums[place, :] = sums[place, :] + (added[h : h + 8] + added[l : l + 8])
        return carry

    lax.fori_loop(0, bins // together, some_bins, 0)
    chunk = lane8 >> 3
    first = lane8 < 64

    def strip(bz, carry):
        for v in range(5):
            pairs = []
            for by in range(8):
                near = sums[pl.ds(pl.multiple_of((bz * 16 + by) * 40 + v * 8, 8), 8), :]
                far = sums[pl.ds(pl.multiple_of((bz * 16 + by + 8) * 40 + v * 8, 8), 8), :]
                pairs.append(jnp.where(first, near + pltpu.roll(near, 64, 1), far + pltpu.roll(far, 64, 1)))
            for j, layer in enumerate(trade_chunks(pairs, chunk)):
                out[pl.ds(v * plane + bz * 8 + j, 8, stride=across), :] = layer
        return carry

    lax.fori_loop(0, 6, strip, 0)


def flow_kernel(gas, sources, x_low, x_high, z_both, y_low, y_high, out, y_ends, x_padded, z_flux):
    row8 = lax.broadcasted_iota(jnp.int32, (8, lanes), 0)
    lane8 = lane_index(8)
    place = jnp.where((row8 == 0) & (lane8 == 0) | (row8 == 1) & (lane8 == lanes - 1), 1.0, 0.0).astype(f32)
    ends = jnp.concatenate([y_low[...], y_high[...], jnp.zeros((6, 5 * plane), f32)], axis=0)
    y_ends[...] = lax.dot_general(
        ends, place, (((0,), (0,)), ((), ())),
        precision=lax.Precision.HIGHEST, preferred_element_type=f32,
    )
    for v in range(5):
        x_padded[v * 480 : v * 480 + across, :] = x_low[v * across : (v + 1) * across, :]
        x_padded[v * 480 + across : v * 480 + 432, :] = gas[v * plane : (v + 1) * plane, :]
        x_padded[v * 480 + 432 : (v + 1) * 480, :] = x_high[v * across : (v + 1) * across, :]
    for side in range(2):
        edge = [z_both[side * 40 + v * 8 : side * 40 + (v + 1) * 8, :] for v in range(5)]
        edge_flux = flux(edge, *primitives(edge), 1)
        for v in range(5):
            z_flux[side * 40 + v * 8 : side * 40 + (v + 1) * 8, :] = edge_flux[v]

    row = lax.broadcasted_iota(jnp.int32, (across, lanes), 0)
    lane = lane_index(across)

    def layer(i, carry):
        def cells(at):
            return [x_padded[pl.ds(pl.multiple_of(v * 480 + at * across, 8), across), :] for v in range(5)]

        def rows(v):
            return pl.ds(pl.multiple_of(v * plane + i * across, 8), across)

        here, below, above = cells(i + 1), cells(i), cells(i + 2)
        u, pressure = primitives(here)
        flux_above = flux(above, *primitives(above), 0)
        flux_below = flux(below, *primitives(below), 0)
        flux_z = flux(here, u, pressure, 1)
        flux_y = flux(here, u, pressure, 2)
        ends = [y_ends[rows(v), :] for v in range(5)]
        flux_ends = flux(ends, *primitives(ends), 2)
        for v in range(5):
            z_low = z_both[pl.ds(40 + v * 8 + i, 1), :]
            z_high = z_both[pl.ds(v * 8 + i, 1), :]
            z_low_flux = z_flux[pl.ds(40 + v * 8 + i, 1), :]
            z_high_flux = z_flux[pl.ds(v * 8 + i, 1), :]

            def z_pair(x, low, high):
                return (
                    jnp.where(row == 0, low, pltpu.roll(x, 1, 0)),
                    jnp.where(row == across - 1, high, pltpu.roll(x, across - 1, 0)),
                )

            def y_pair(x, end):
                return (
                    jnp.where(lane == 0, end, pltpu.roll(x, 1, 1)),
                    jnp.where(lane == lanes - 1, end, pltpu.roll(x, lanes - 1, 1)),
                )

            z_down, z_up = z_pair(here[v], z_low, z_high)
            z_flux_down, z_flux_up = z_pair(flux_z[v], z_low_flux, z_high_flux)
            y_down, y_up = y_pair(here[v], ends[v])
            y_flux_down, y_flux_up = y_pair(flux_y[v], flux_ends[v])
            spread = (below[v] + above[v]) + (z_down + z_up) + (y_down + y_up) - 6.0 * here[v]
            change = (flux_above[v] - flux_below[v]) + (z_flux_up - z_flux_down) + (y_flux_up - y_flux_down)
            flow = 0.5 * change - 1.5 * spread
            out[rows(v), :] = here[v] - 0.1 * flow + sources[rows(v), :]
        return carry

    lax.fori_loop(0, depth, layer, 0)


def leave_kernel(returned, drops, crossing, updated, toward_next, toward_previous):
    for g in range(bins // 8):
        values = group_values(returned, g)
        places = [drops[pl.ds(g * 64 + a, 8, stride=8), :] + 0.2 * values[a] for a in range(3)]
        for n, value in enumerate(places + values):
            updated[n * bins + g * 8 : n * bins + g * 8 + 8, :] = value
    row = lax.broadcasted_iota(jnp.int32, (bins, moving), 0)
    dims = (((0,), (0,)), ((), ()))
    for side, out in ((0, toward_next), (1, toward_previous)):
        slots = crossing[side : side + 1, :]
        in_bin = jnp.where(row == (slots >> 7), 1.0, 0.0).astype(bf16)
        in_lane = row == (slots & (lanes - 1))
        for n in range(8):
            high, low = split(updated[n * bins : (n + 1) * bins, :])
            picked = lax.dot_general(high, in_bin, dims, preferred_element_type=f32)
            picked += lax.dot_general(low, in_bin, dims, preferred_element_type=f32)
            out[n : n + 1, :] = jnp.sum(jnp.where(in_lane, picked, 0.0), axis=0, keepdims=True)


def stay_kernel(updated, keep, out, staying, sems):
    copies = []
    for n in range(quarters):
        for g in range(n * 4, n * 4 + 4):
            mask = keep[g * 8 : (g + 1) * 8, :]
            for v in range(8):
                plane_rows = updated[v * bins + g * 8 : v * bins + g * 8 + 8, :]
                staying[pl.ds(g * 64 + v, 8, stride=8), :] = plane_rows * mask
        part = pl.ds(n * 256, 256)
        copies.append(pltpu.make_async_copy(staying.at[part], out.at[part], sems.at[n]))
        copies[n].start()
    for copy in copies:
        copy.wait()


def shape(rows, columns=lanes, dtype=f32):
    return jax.ShapeDtypeStruct((rows, columns), dtype)


def shifted_by(x, axis, by):
    count = lax.axis_size(axis)
    return lax.ppermute(x, axis, [(i, (i + by) % count) for i in range(count)])


def exchange(x):
    return lax.all_to_all(x, "gx", split_axis=0, concat_axis=0, tiled=True)


def call(kernel, out_shape, in_specs, mib, scratch=(), out_specs=None):
    if out_specs is None:
        out_specs = [vmem] * len(out_shape) if isinstance(out_shape, list) else vmem
    return pl.pallas_call(
        kernel, name=kernel.__name__, out_shape=out_shape, in_specs=in_specs,
        out_specs=out_specs, scratch_shapes=list(scratch), compiler_params=params(mib),
    )


def pack(drops, bin_blocks, bin_counts):
    return call(
        pack_kernel, jax.ShapeDtypeStruct((peers * tiles_out, 4, lanes), f32), [hbm] * 3, 60,
        [pltpu.VMEM((bins * 8, lanes), f32), pltpu.VMEM((2, 1, lanes), jnp.int32), pltpu.SemaphoreType.DMA((3,))],
    )(drops, bin_blocks.reshape(1, bins), bin_counts.reshape(1, bins))


def faces(gas, crossing, bin_counts):
    return call(
        face_kernel,
        [shape(240), shape(240), shape(80), shape(1, 1920), shape(1, 1920), shape(bins)], [vmem] * 3, 16,
    )(gas, crossing, bin_counts.reshape(1, bins))


def make_table(gas):
    return call(table_kernel, shape(blocks * block_rows, dtype=bf16), [vmem], 24)(gas)


unpack_scratch = [
    pltpu.VMEM((bins * 8, lanes), f32), pltpu.VMEM((4, lanes), jnp.int32), pltpu.SMEM((4, lanes), jnp.int32),
]


answer_shape = (peers * 5, 4, lanes)


def sample(received, table):
    return call(
        sample_kernel, pltpu.HBM(answer_shape, f32), [vmem] * 2, 24,
        unpack_scratch
        + [pltpu.VMEM((bins * 40, lanes), f32), pltpu.VMEM(answer_shape, f32),
           pltpu.SemaphoreType.DMA((quarters + 1,))],
        hbm,
    )(received, table)


def deposit(results, received):
    return call(
        deposit_kernel, shape(5 * plane), [hbm, vmem], 24,
        [pltpu.VMEM(answer_shape, f32)] + unpack_scratch
        + [pltpu.VMEM((blocks * 40, lanes), f32), pltpu.VMEM((bins * 8, lanes), f32),
           pltpu.SemaphoreType.DMA((2,))],
    )(pltpu.with_memory_space_constraint(results, pltpu.HBM), received)


def advance(gas, sources, halos):
    return call(
        flow_kernel, shape(5 * plane), [vmem] * 7, 24,
        [pltpu.VMEM((5 * plane, lanes), f32), pltpu.VMEM((2400, lanes), f32), pltpu.VMEM((80, lanes), f32)],
    )(gas, sources, *halos)


def leave(returned, drops, crossing):
    return call(
        leave_kernel, [shape(bins * 8), shape(8, moving), shape(8, moving)], [vmem] * 3, 16
    )(returned, drops, crossing)


def stay(updated, keep):
    return call(
        stay_kernel, shape(bins * 8), [vmem, vmem], 16,
        [pltpu.VMEM((bins * 8, lanes), f32), pltpu.SemaphoreType.DMA((quarters,))], hbm,
    )(updated, keep)


def per_device(gas_state, droplets, bin_blocks, bin_counts, crossing):
    gas = gas_state.reshape(5 * plane, lanes)
    drops = droplets.reshape(8, bins, lanes).transpose(1, 0, 2).reshape(bins * 8, lanes)
    received = exchange(pack(drops, bin_blocks, bin_counts))

    x_low, x_high, z_both, y_low, y_high, keep = faces(gas, crossing, bin_counts)
    halos = (
        shifted_by(x_high, "gx", 1),
        shifted_by(x_low, "gx", -1),
        shifted_by(z_both, "grp", 1),
        shifted_by(y_high, "gy", 1),
        shifted_by(y_low, "gy", -1),
    )
    table = make_table(gas)
    received, halos_z, halos_y1, halos_y2 = lax.optimization_barrier((received,) + halos[2:])
    results = sample(received, table)
    results, halo_x1, halo_x2 = lax.optimization_barrier((results,) + halos[:2])
    halos = (halo_x1, halo_x2, halos_z, halos_y1, halos_y2)
    returned = exchange(results)
    gas_next = advance(gas, deposit(results, received), halos)
    returned, gas_next = lax.optimization_barrier((returned, gas_next))
    updated, toward_next, toward_previous = leave(returned, drops, crossing)
    from_previous = shifted_by(toward_next, "gx", 1)
    from_next = shifted_by(toward_previous, "gx", -1)
    arrivals = jnp.stack([from_previous, from_next], axis=1)
    kept = stay(updated, keep)
    droplets_next = kept.reshape(bins, 8, lanes).transpose(1, 0, 2).reshape(8, bins * lanes)
    return gas_next.reshape(gas_state.shape), droplets_next, arrivals


def solution(mesh):
    whole = ("grp", "gx", "gy")
    in_specs = (P(None, "gx", "grp", "gy"), P(None, whole), P(whole), P(whole), P(None, whole))
    out_specs = (P(None, "gx", "grp", "gy"), P(None, whole), P(None, None, whole))
    return jax.shard_map(per_device, mesh=mesh, in_specs=in_specs, out_specs=out_specs, check_vma=False)
```
